32 devices in a mesh: row: 4 (over z), col: 8 (over y, x, core).
Axes of the slice: x: 2, y: 2, z: 4, core: 2. Of those that a mesh axis runs over, the one named last changes fastest.
Arguments:
- hidden_in: bfloat16 [1024, 1792], P('col', 'row'), may hold values from -6 to 6
- attn_gain: float32 [1792], replicated, may hold values from 0.1 to 1.9
- mlp_gain: float32 [1792], replicated, may hold values from 0.1 to 1.9
- w_query: bfloat16 [1792, 256], P(None, 'row'), may hold values from -0.125 to 0.125
- w_key: bfloat16 [1792, 256], P(None, 'row'), may hold values from -0.125 to 0.125
- w_value: bfloat16 [1792, 1792], P(None, 'row'), may hold values from -0.125 to 0.125
- w_out: bfloat16 [1792, 1792], P('row'), may hold values from -0.1875 to 0.1875
- w_gate: bfloat16 [1792, 3584], P(None, 'row'), may hold values from -0.125 to 0.125
- w_up: bfloat16 [1792, 3584], P(None, 'row'), may hold values from -0.125 to 0.125
- w_down: bfloat16 [3584, 1792], P('row'), may hold values from -0.125 to 0.125
- page_states: bfloat16 [128, 16, 273, 112], P('col', 'row'), may hold values from -16 to 16
- page_norms: float32 [128, 16, 273], P('col', 'row'), as said below
- page_home: int32 [128, 1], P('col'), may hold values from 0 to 7; in each aligned block of 16 rows (0 to 15, 16 to 31, ...) at most 4 rows name the same one
- page_request: int32 [128], P('col'), may hold values from 0 to 1
- parents: int32 [16, 64], P('col'), may hold values from 0 to 62, as said below
- accepted: int32 [16], P('col'), may hold values from 0 to 63
Outputs:
- hidden_out: bfloat16 [1024, 1792], P('col', 'row')
- new_states: bfloat16 [16, 16, 273, 112], P('col', 'row')
- new_norms: float32 [16, 16, 273], P('col', 'row')
The draws below stay inside these ranges and needn't reach their ends.
Inputs may be any that keep to these rules, and one draw needn't show every extreme that they name: Among the 16 slots of one device at most 4 have the same page_home, and in every draw some device has exactly 4. parents[r, 0] = 0, parents[r, i] < i for i >= 1, and the last node's parent is the node before it. Each page_norms[s, h] is a factor of 2 to 16 times the mean of phi over eight vectors, so phi(u) . page_norms[s, h] >= 1 for every vector u.
All inputs are finite; a program needn't handle non-finite values.
Results may differ from the reference program's by a relative error of at most 0.023.
Values may be sent and summed in bfloat16 or wider, within the bound.
A program may use at most 128 MiB of HBM per device.

```python
import math
import jax
import jax.numpy as jnp
import numpy as np
from jax import lax

D = 1792
H = 16
FD = 16
DV = 112
F = 273
FF = 3584
NODES = 64
REQ_DEV = 2
SLOTS_DEV = 16
CAP = 4
REQS = 16
SLOTS = 128
TOKENS = 1024
N_ROW = 4
N_COL = 8


def feature_map_drawn(vectors):
    width_in = vectors.shape[-1]
    linear = vectors * width_in ** (-0.25)
    square = vectors[..., :, None] * vectors[..., None, :] * (2.0 * width_in) ** (-0.5)
    square = square.reshape(vectors.shape[:-1] + (width_in * width_in,))
    leading = jnp.ones(vectors.shape[:-1] + (1,), vectors.dtype)
    return jnp.concatenate([leading, linear, square], axis=-1)


def draw_page_norms(key, part):
    key_vectors, key_factor = jax.random.split(jax.random.fold_in(key, 11))
    samples = jax.random.normal(key_vectors, (SLOTS, H, 8, FD), jnp.float32)
    factor = jax.random.uniform(key_factor, (SLOTS, H, 1), jnp.float32, 2.0, 16.0)
    return jnp.mean(feature_map_drawn(samples), axis=2) * factor


def draw_parents(key, part):
    node_ids = jnp.arange(NODES, dtype=jnp.int32)
    upper_bound = jnp.maximum(node_ids, 1)
    picked = jax.random.randint(jax.random.fold_in(key, 23), (REQS, NODES), 0, upper_bound[None, :])
    picked = jnp.where(node_ids[None, :] == NODES - 1, NODES - 2, picked)
    return jnp.where(node_ids[None, :] == 0, 0, picked).astype(jnp.int32)


def with_ends(result, rng, low, top_value):
    index_at = [jax.random.randint(jax.random.fold_in(rng, axis), (), 0, length) for axis, length in enumerate(result.shape)]
    main_axis = result.shape.index(max(result.shape))
    next_to = index_at[:main_axis] + [(index_at[main_axis] + 1) % result.shape[main_axis]] + index_at[main_axis + 1:]
    return result.at[tuple(index_at)].set(low).at[tuple(next_to)].set(top_value)


def spiked(entries, own_key, source, target, blocks, factor):
    owner, partner = [(jnp.arange(entries.shape[dim]) // (entries.shape[dim] // blocks)).reshape([-1 if axis == dim else 1 for axis in range(entries.ndim)]) for dim in (source, target)]
    chosen = jax.random.permutation(own_key, blocks)[partner]
    strong = (owner == chosen) | (owner == (partner + blocks // 2) % blocks)
    return jnp.where(strong, factor * entries, entries)


def steps_of(key, shape, shards, low, largest):
    loudness = 1.0
    for dim, parts in shards:
        steps = jax.random.uniform(jax.random.fold_in(jax.random.fold_in(key, 6), dim), (parts,), jnp.float32, low / len(shards), largest / len(shards))
        loudness = loudness * jnp.repeat(jnp.exp(steps), shape[dim] // parts).reshape((-1,) + (1,) * (len(shape) - 1 - dim))
    return loudness


def deal_out(stream_key, own, number, rows, number_of, top, limit, slope):
    ranking = jax.random.permutation(stream_key, number_of)
    crowded, usual = shares(number_of, rows * top, limit, slope, True), shares(number_of, rows * top, limit, slope, False)
    places = jnp.arange(number_of)

    def named(lengths, turn):
        used = int((lengths > 0).sum())
        fixed = max(1, used // 4)
        moved = fixed + (places - fixed + turn * (used - fixed)) % max(1, number_of - fixed)
        return jnp.zeros((number_of,), jnp.int32).at[ranking[jnp.where(places < fixed, places, moved)]].set(jnp.asarray(lengths, jnp.int32))

    lengths = jnp.where(number % 4 == 0, named(crowded, number // 4), named(usual, number - number // 4 - 1))
    mixed = jax.random.permutation(jax.random.fold_in(own, 3), number_of)
    donor, receiver = mixed[0:number_of // 2 * 2:2], mixed[1:number_of // 2 * 2:2]
    room = jnp.minimum(lengths[donor] - 1, limit - lengths[receiver]) // 2
    room = jnp.where((donor == ranking[0]) | (receiver == ranking[0]) | (lengths[receiver] == 0), 0, jnp.maximum(room, 0))
    moved = jax.random.randint(jax.random.fold_in(own, 4), (number_of // 2,), 0, 1 << 20) % (room + 1)
    lengths = lengths.at[donor].add(-moved).at[receiver].add(moved)
    members = jnp.searchsorted(jnp.cumsum(lengths), jnp.arange(rows * top), side="right").astype(jnp.int32)
    table = members.reshape(top, rows).T
    table = table[jax.random.permutation(jax.random.fold_in(own, 1), rows)]
    turn = jax.random.randint(jax.random.fold_in(own, 2), (rows, 1), 0, top)
    return jnp.take_along_axis(table, (jnp.arange(top)[None, :] + turn) % top, axis=1)


def shares(count, total, limit, slope, full):
    portions = [(1 << 20) // math.isqrt(grade ** slope) + 1 for grade in range(1, count + 1)]
    largest = limit if full else min(limit, max(-(-total // count), total * portions[0] // sum(portions)))
    least = 1 if total - largest >= count - 1 else 0
    counts, rest = [largest] + [least] * (count - 1), total - largest - least * (count - 1)
    while rest > 0:
        free = [i for i in range(1, count) if counts[i] < largest] or [i for i in range(1, count) if counts[i] < limit]
        pool, left = sum([portions[i] for i in free]), rest
        for i in free:
            more = min(limit - counts[i], max(1, left * portions[i] // pool), rest)
            counts[i] = counts[i] + more
            rest = rest - more
    return np.array(counts)


def scatter_about(key, dims, deviation, limit, cuts=(), kind=jnp.bfloat16):
    drawn = jax.random.normal(key, dims, jnp.float32) * deviation
    if len(cuts) > 0:
        drawn = steps_of(key, dims, cuts, -0.22, 0.18) * drawn
    return jnp.clip(drawn, min=-limit, max=limit).astype(kind)


def bell_draw_with(rng, dims, spread, limit, pieces, heavy, kind=jnp.bfloat16):
    array = spread * jax.random.normal(rng, dims, jnp.float32)
    if pieces:
        array = array * steps_of(rng, dims, pieces, -0.22, 0.18)
    return jnp.clip(spiked(array, jax.random.fold_in(rng, 3), *heavy), -limit, limit).astype(kind)


def setup_inputs(seed: int = 0) -> dict:
    splits = jax.random.split(jax.random.key(seed), 17)
    hidden_in = scatter_about(splits[0], (TOKENS, D), 1.0, 6.0, ((0, 8), (1, 4)))
    attn_gain = jnp.clip(1.0 + 0.18 * jax.random.normal(splits[1], (D,), jnp.float32), 0.1, 1.9)
    mlp_gain = jnp.clip(1.0 + 0.18 * jax.random.normal(splits[2], (D,), jnp.float32), 0.1, 1.9)
    w_query = scatter_about(splits[3], (D, H * FD), D ** -0.5, 0.125, ((1, 4),))
    w_key = scatter_about(splits[4], (D, H * FD), D ** -0.5, 0.125, ((1, 4),))
    w_value = scatter_about(splits[5], (D, H * DV), D ** -0.5, 0.125, ((1, 4),))
    w_out = bell_draw_with(splits[6], (H * DV, D), (H * DV) ** -0.5, 0.1875, ((0, 4),), (0, 1, 4, 2.0))
    w_gate = scatter_about(splits[7], (D, FF), D ** -0.5, 0.125, ((1, 4),))
    w_up = scatter_about(splits[8], (D, FF), D ** -0.5, 0.125, ((1, 4),))
    w_down = bell_draw_with(splits[9], (FF, D), FF ** -0.5, 0.125, ((0, 4),), (0, 1, 4, 2.0))
    page_states = scatter_about(splits[10], (SLOTS, H, F, DV), 4.0, 16.0, ((0, 8), (1, 4)))
    page_norms = draw_page_norms(jax.random.fold_in(splits[16], 71), 0)
    page_home_keys = jax.random.split(jax.random.fold_in(splits[12], 1), SLOTS // SLOTS_DEV)
    page_home_turns = jax.random.permutation(jax.random.fold_in(splits[12], 3), SLOTS // SLOTS_DEV)
    page_home = jax.vmap(lambda own, number: deal_out(jax.random.fold_in(splits[12], 2), own, number, SLOTS_DEV, N_COL, 1, CAP, 2))(page_home_keys, page_home_turns).reshape((SLOTS, 1))
    page_request = with_ends(jax.random.randint(splits[13], (SLOTS,), 0, REQ_DEV), jax.random.fold_in(splits[13], 1), 0, REQ_DEV - 1).astype(jnp.int32)
    parents = draw_parents(jax.random.fold_in(splits[16], 71), 0)
    accepted = with_ends(jax.random.randint(splits[15], (REQS,), 0, NODES), jax.random.fold_in(splits[15], 1), 0, NODES - 1).astype(jnp.int32)
    return dict(hidden_in=hidden_in, attn_gain=attn_gain, mlp_gain=mlp_gain, w_query=w_query, w_key=w_key, w_value=w_value, w_out=w_out, w_gate=w_gate, w_up=w_up, w_down=w_down, page_states=page_states, page_norms=page_norms, page_home=page_home, page_request=page_request, parents=parents, accepted=accepted)


epsilon = 1e-05

def feature_map(vectors):
    width_in = vectors.shape[-1]
    linear = vectors * width_in ** (-0.25)
    square = vectors[..., :, None] * vectors[..., None, :] * (2.0 * width_in) ** (-0.5)
    square = square.reshape(vectors.shape[:-1] + (width_in * width_in,))
    leading = jnp.ones(vectors.shape[:-1] + (1,), vectors.dtype)
    return jnp.concatenate([leading, linear, square], axis=-1)

def rms_norm(hidden, gain):
    mean_square = lax.optimization_barrier(jnp.mean(hidden * hidden, axis=-1, keepdims=True))
    return hidden * lax.rsqrt(mean_square + epsilon) * gain

def ancestors(parents):
    nodes = parents.shape[-1]
    node_ids = jnp.arange(nodes, dtype=jnp.int32)
    linked = (parents[..., :, None] == node_ids[None, :]) | (node_ids[:, None] == node_ids[None, :])
    reached = linked.astype(jnp.float32)
    for repeat in range(max(1, (nodes - 1).bit_length())):
        reached = jnp.minimum(jnp.einsum('rij,rjk->rik', reached, reached, precision=lax.Precision.HIGHEST), 1.0)
    return reached

def project_groups(inputs, weight, groups):
    block_width = inputs.shape[1] // groups
    summed = jnp.zeros((inputs.shape[0], weight.shape[1]), jnp.float32)
    for group_index in range(groups):
        lower = group_index * block_width
        partial_value = jnp.dot(inputs[:, lower:lower + block_width], weight[lower:lower + block_width], preferred_element_type=jnp.float32)
        summed = summed + lax.optimization_barrier(partial_value.astype(jnp.bfloat16)).astype(jnp.float32)
    return summed

def reference(hidden_in, attn_gain, mlp_gain, w_query, w_key, w_value, w_out, w_gate, w_up, w_down, page_states, page_norms, page_home, page_request, parents, accepted):
    highest = lax.Precision.HIGHEST
    hidden = hidden_in.astype(jnp.float32)
    normed = rms_norm(hidden, attn_gain).astype(jnp.bfloat16)
    queries = jnp.dot(normed, w_query, preferred_element_type=jnp.float32).astype(jnp.bfloat16)
    key_rows = jnp.dot(normed, w_key, preferred_element_type=jnp.float32).astype(jnp.bfloat16)
    values = jnp.dot(normed, w_value, preferred_element_type=jnp.float32).astype(jnp.bfloat16)
    query_heads = queries.astype(jnp.float32).reshape(REQS, NODES, H, FD)
    key_heads = key_rows.astype(jnp.float32).reshape(REQS, NODES, H, FD)
    value_heads = values.astype(jnp.float32).reshape(REQS, NODES, H, DV)
    reached = ancestors(parents)
    scaled = jnp.einsum('rihf,rjhf->rhij', query_heads, key_heads, precision=highest) / math.sqrt(FD)
    kernel = (1.0 + scaled + 0.5 * scaled * scaled) * reached[:, None, :, :]
    tree_den = jnp.transpose(lax.optimization_barrier(jnp.sum(kernel, axis=-1)), (0, 2, 1))
    kernel_low = lax.optimization_barrier(kernel.astype(jnp.bfloat16)).astype(jnp.float32)
    tree_num = jnp.einsum('rhij,rjhd->rihd', kernel_low, value_heads, precision=highest)
    phi_query = feature_map(query_heads)
    phi_low = lax.optimization_barrier(phi_query.astype(jnp.bfloat16)).astype(jnp.float32)
    owners = (page_home[:, 0] * REQ_DEV + page_request).astype(jnp.int32)

    def add_page(carry, slot_data):
        num_total, den_total = carry
        state, norm_row, owner = slot_data
        rows_low = lax.dynamic_index_in_dim(phi_low, owner, 0, keepdims=False)
        rows_full = lax.dynamic_index_in_dim(phi_query, owner, 0, keepdims=False)
        numer = jnp.einsum('nhf,hfd->nhd', rows_low, state.astype(jnp.float32), precision=highest)
        denom = jnp.einsum('nhf,hf->nh', rows_full, norm_row, precision=highest)
        return ((num_total.at[owner].add(numer), den_total.at[owner].add(denom)), None)
    zero_num = jnp.zeros((REQS, NODES, H, DV), jnp.float32)
    zero_den = jnp.zeros((REQS, NODES, H), jnp.float32)
    (pref_num, pref_den), unused = lax.scan(add_page, (zero_num, zero_den), (page_states, page_norms, owners))
    mixed = ((pref_num + tree_num) / (pref_den + tree_den)[..., None]).astype(jnp.bfloat16)
    mixed = mixed.reshape(TOKENS, H * DV)
    attn = project_groups(mixed, w_out, N_ROW)
    residual = hidden + attn
    normed_mlp = rms_norm(residual, mlp_gain).astype(jnp.bfloat16)
    gate_proj = jnp.dot(normed_mlp, w_gate, preferred_element_type=jnp.float32)
    up_proj = jnp.dot(normed_mlp, w_up, preferred_element_type=jnp.float32)
    activated = (jax.nn.silu(gate_proj) * up_proj).astype(jnp.bfloat16)
    mlp_out = project_groups(activated, w_down, N_ROW)
    hidden_out = (residual + mlp_out).astype(jnp.bfloat16)
    node_ids = jnp.arange(NODES, dtype=jnp.int32)
    chosen = (node_ids[None, :] == accepted[:, None]).astype(jnp.float32)
    path_mask = jnp.einsum('ri,rij->rj', chosen, reached, precision=highest)
    phi_key = feature_map(key_heads)
    new_norms = jnp.einsum('rj,rjhf->rhf', path_mask, phi_key, precision=highest)
    phi_key_low = lax.optimization_barrier(phi_key.astype(jnp.bfloat16)).astype(jnp.float32)
    weighted = phi_key_low * path_mask[:, :, None, None]
    new_states = jnp.einsum('rjhf,rjhd->rhfd', weighted, value_heads, precision=highest).astype(jnp.bfloat16)
    return (hidden_out, new_states, new_norms)
```

```python
import functools
import math

import jax
import jax.numpy as jnp
import numpy as np
from jax import lax
from jax.experimental import pallas as pl
from jax.experimental.pallas import tpu as pltpu
from jax.sharding import PartitionSpec as P

epsilon = 1e-05


def feature_map(vectors):
    width_in = vectors.shape[-1]
    linear = vectors * width_in ** (-0.25)
    square = vectors[..., :, None] * vectors[..., None, :] * (2.0 * width_in) ** (-0.5)
    square = square.reshape(vectors.shape[:-1] + (width_in * width_in,))
    leading = jnp.ones(vectors.shape[:-1] + (1,), vectors.dtype)
    return jnp.concatenate([leading, linear, square], axis=-1)


def rms_norm(hidden, gain):
    mean_square = jnp.mean(hidden * hidden, axis=-1, keepdims=True)
    return hidden * lax.rsqrt(mean_square + epsilon) * gain


def ancestors(parents):
    nodes = parents.shape[-1]
    node_ids = jnp.arange(nodes, dtype=jnp.int32)
    linked = (parents[..., :, None] == node_ids[None, :]) | (node_ids[:, None] == node_ids[None, :])
    reached = linked.astype(jnp.float32)
    for repeat in range(max(1, (nodes - 1).bit_length())):
        reached = jnp.minimum(
            jnp.einsum("rij,rjk->rik", reached, reached, precision=lax.Precision.HIGHEST), 1.0
        )
    return reached


def pack_slots(homes, requests, col_count, capacity):
    slot_count = homes.shape[0]
    slot_ids = jnp.arange(slot_count, dtype=jnp.int32)
    same_home = (homes[:, None] == homes[None, :]) & (slot_ids[None, :] < slot_ids[:, None])
    ranks = jnp.sum(same_home.astype(jnp.int32), axis=1)
    places = homes * capacity + ranks
    targets = jnp.arange(col_count * capacity, dtype=jnp.int32)
    packer = (targets[:, None] == places[None, :]).astype(jnp.float32)
    labels = (
        jnp.dot(packer, (requests + 1).astype(jnp.float32), precision=lax.Precision.HIGHEST) - 1.0
    )
    return (packer, labels)


def local(
    hidden_in,
    attn_gain,
    mlp_gain,
    w_query,
    w_key,
    w_value,
    w_out,
    w_gate,
    w_up,
    w_down,
    page_states,
    page_norms,
    page_home,
    page_request,
    parents,
    accepted,
):
    highest = lax.Precision.HIGHEST
    local_heads = page_states.shape[1]
    feat_width = w_query.shape[1] // local_heads
    value_width = w_value.shape[1] // local_heads
    req_local = parents.shape[0]
    nodes = parents.shape[1]
    tok_local = hidden_in.shape[0]
    slot_count = page_states.shape[0]
    col_count = lax.axis_size("col")
    row_count = lax.axis_size("row")
    capacity = max(2, 2 * slot_count // col_count)
    row_index = lax.axis_index("row")
    gathered = lax.all_gather(hidden_in, "row", axis=1, tiled=True)
    hidden = gathered.astype(jnp.float32)
    normed = rms_norm(hidden, attn_gain).astype(jnp.bfloat16)
    queries = jnp.dot(normed, w_query, preferred_element_type=jnp.float32).astype(jnp.bfloat16)
    key_rows = jnp.dot(normed, w_key, preferred_element_type=jnp.float32).astype(jnp.bfloat16)
    values = jnp.dot(normed, w_value, preferred_element_type=jnp.float32).astype(jnp.bfloat16)
    query_heads = queries.reshape(req_local, nodes, local_heads, feat_width)
    key_heads = key_rows.reshape(req_local, nodes, local_heads, feat_width)
    value_heads = values.reshape(req_local, nodes, local_heads, value_width)
    reached = ancestors(parents)
    scaled = jnp.einsum(
        "rihf,rjhf->rhij", query_heads, key_heads, preferred_element_type=jnp.float32
    ) / math.sqrt(feat_width)
    kernel = (1.0 + scaled + 0.5 * scaled * scaled) * reached[:, None, :, :]
    tree_den = jnp.transpose(jnp.sum(kernel, axis=-1), (0, 2, 1))
    tree_num = jnp.einsum(
        "rhij,rjhd->rihd",
        kernel.astype(jnp.bfloat16),
        value_heads,
        preferred_element_type=jnp.float32,
    )
    homes = page_home[:, 0]
    packer, packed_ids = pack_slots(homes, page_request, col_count, capacity)
    request_ids = jnp.arange(req_local, dtype=jnp.float32)
    sent_states = jnp.einsum(
        "ps,shfd->phfd",
        packer.astype(jnp.bfloat16),
        page_states,
        preferred_element_type=jnp.float32,
    ).astype(jnp.bfloat16)
    sent_norms = jnp.einsum("ps,shf->phf", packer, page_norms, precision=highest)
    got_states = lax.all_to_all(sent_states, "col", split_axis=0, concat_axis=0, tiled=True)
    got_norms, got_ids = (
        lax.all_to_all(
            sent_norms.astype(jnp.bfloat16), "col", split_axis=0, concat_axis=0, tiled=True
        ).astype(sent_norms.dtype),
        lax.all_to_all(
            packed_ids.astype(jnp.bfloat16), "col", split_axis=0, concat_axis=0, tiled=True
        ).astype(packed_ids.dtype),
    )
    unpack = (got_ids[None, :] == request_ids[:, None]).astype(jnp.float32)
    phi_query = feature_map(query_heads.astype(jnp.float32))
    phi_select = jnp.einsum(
        "rp,rnhf->pnhf",
        unpack.astype(jnp.bfloat16),
        phi_query.astype(jnp.bfloat16),
        preferred_element_type=jnp.float32,
    ).astype(jnp.bfloat16)
    phi_full = jnp.einsum("rp,rnhf->pnhf", unpack, phi_query, precision=highest)
    slot_num = jnp.einsum(
        "pnhf,phfd->pnhd", phi_select, got_states, preferred_element_type=jnp.float32
    )
    slot_den = jnp.einsum("pnhf,phf->pnh", phi_full, got_norms, precision=highest)
    pref_num = jnp.einsum("rp,pnhd->rnhd", unpack, slot_num, precision=highest)
    pref_den = jnp.einsum("rp,pnh->rnh", unpack, slot_den, precision=highest)
    mixed = ((pref_num + tree_num) / (pref_den + tree_den)[..., None]).astype(jnp.bfloat16)
    mixed = mixed.reshape(tok_local, local_heads * value_width)
    partial_value = jnp.dot(mixed, w_out, preferred_element_type=jnp.float32)
    feature_count = partial_value.shape[1]
    share = feature_count // row_count
    attn_all = lax.psum(partial_value.astype(jnp.bfloat16), "row").astype(jnp.float32)
    residual_all = hidden + attn_all
    normed_mlp = rms_norm(residual_all, mlp_gain).astype(jnp.bfloat16)
    residual = lax.dynamic_slice_in_dim(residual_all, row_index * share, share, 1)
    gate_proj = jnp.dot(normed_mlp, w_gate, preferred_element_type=jnp.float32)
    up_proj = jnp.dot(normed_mlp, w_up, preferred_element_type=jnp.float32)
    activated = (jax.nn.silu(gate_proj) * up_proj).astype(jnp.bfloat16)
    mlp_share = lax.psum_scatter(
        jnp.einsum("fd,tf->dt", w_down, activated, preferred_element_type=jnp.float32).astype(
            jnp.bfloat16
        ),
        "row",
        scatter_dimension=0,
        tiled=True,
    ).astype(jnp.float32)
    hidden_out = (residual + jnp.transpose(mlp_share)).astype(jnp.bfloat16)
    node_ids = jnp.arange(nodes, dtype=jnp.int32)
    chosen = (node_ids[None, :] == accepted[:, None]).astype(jnp.float32)
    path_mask = jnp.einsum("ri,rij->rj", chosen, reached, precision=highest)
    phi_key = feature_map(key_heads.astype(jnp.float32))
    new_norms = jnp.einsum("rj,rjhf->rhf", path_mask, phi_key, precision=highest)
    weighted = phi_key.astype(jnp.bfloat16) * path_mask.astype(jnp.bfloat16)[:, :, None, None]
    new_states = jnp.einsum(
        "rjhf,rjhd->rhfd", weighted, value_heads, preferred_element_type=jnp.float32
    ).astype(jnp.bfloat16)
    return (hidden_out, new_states, new_norms)

MESH_KEYS = ("row", "col")


def expansion(heads, feat_width, shifts, window):
    count = heads * (1 + feat_width + feat_width * feat_width)
    first = np.zeros((len(shifts), 128, window), np.float32)
    second = np.zeros((len(shifts), 128, window), np.float32)
    scale = np.zeros((len(shifts), 1, window), np.float32)
    unit = heads * feat_width
    for index, shift in enumerate(shifts):
        for t in range(count):
            f, h = divmod(t, heads)
            column = shift + t
            if f == 0:
                a, b, c = unit + h, unit + h, 1.0
            elif f <= feat_width:
                a, b, c = h * feat_width + f - 1, unit + h, feat_width ** (-0.25)
            else:
                i, j = divmod(f - 1 - feat_width, feat_width)
                a, b, c = h * feat_width + i, h * feat_width + j, (2.0 * feat_width) ** (-0.5)
            first[index, a, column] = 1.0
            second[index, b, column] = 1.0
            scale[index, 0, column] = c
    return first, second, scale


def peers_of(axis):
    size, me = lax.axis_size(axis), lax.axis_index(axis)
    return [lax.rem(me + step, size) for step in range(1, size)]


def greet():
    barrier = pltpu.get_barrier_semaphore()
    count = 0
    for axis in MESH_KEYS:
        for peer in peers_of(axis):
            pl.semaphore_signal(
                barrier, inc=1, device_id={axis: peer}, device_id_type=pl.DeviceIdType.MESH
            )
            count += 1
    pl.semaphore_wait(barrier, count)


def push(axis, source_of, target, send_sem, recv_sem):
    copies = []
    for step, peer in enumerate(peers_of(axis)):
        copy = pltpu.make_async_remote_copy(
            src_ref=source_of(peer),
            dst_ref=target,
            send_sem=send_sem.at[step],
            recv_sem=recv_sem.at[step],
            device_id={axis: peer},
            device_id_type=pl.DeviceIdType.MESH,
        )
        copy.start()
        copies.append(copy)
    return copies


def extended(rows_t, heads):
    unit = rows_t.shape[0]
    ids = lax.broadcasted_iota(jnp.int32, (128 - unit, rows_t.shape[1]), 0)
    ones = jnp.where(ids < heads, 1.0, 0.0)
    return jnp.concatenate([rows_t, ones], axis=0)


def project_kernel(
    heads, hidden_ref, gain_ref, wq_any, wk_any, wv_any,
    hidden_out, q_out, qall_out, k_out, v_out,
    wq, wk, wv, hid, normed, qext, qall, w_sem, hs_sem, hr_sem, qs_sem, qr_sem,
):
    me_row, me_col = lax.axis_index("row"), lax.axis_index("col")
    share, tokens = hidden_ref.shape
    loads = [
        pltpu.make_async_copy(src, dst, w_sem.at[i])
        for i, (src, dst) in enumerate(((wq_any, wq), (wk_any, wk), (wv_any, wv)))
    ]
    for load in loads:
        load.start()
    greet()
    mine = hid.at[pl.ds(pl.multiple_of(me_row * share, 16), share)]
    copies = push("row", lambda peer: hidden_ref, mine, hs_sem, hr_sem)
    mine[...] = hidden_ref[...]
    gain_t = jnp.transpose(gain_ref[...])
    for copy in copies:
        copy.wait_recv()
    width = hid.shape[0]
    total = jnp.zeros((1, tokens), jnp.float32)
    for j in range(width // 128):
        x = hid[128 * j : 128 * j + 128, :].astype(jnp.float32)
        total += jnp.sum(x * x, axis=0, keepdims=True)
    inverse = lax.rsqrt(total / width + epsilon)
    for j in range(width // 128):
        x = hid[128 * j : 128 * j + 128, :].astype(jnp.float32)
        normed[128 * j : 128 * j + 128, :] = (x * inverse * gain_t[:, j : j + 1]).astype(jnp.bfloat16)
    for load in loads:
        load.wait()
    q_t = jnp.dot(wq[...], normed[...], preferred_element_type=jnp.float32)
    q_t = q_t.astype(jnp.bfloat16).astype(jnp.float32)
    qext[...] = jnp.transpose(extended(q_t, heads)).astype(jnp.bfloat16)
    own = qall.at[pl.ds(pl.multiple_of(me_col * tokens, 16), tokens)]
    q_copies = push("col", lambda peer: qext, own, qs_sem, qr_sem)
    own[...] = qext[...]
    q_out[...] = qext[...]
    k_t = jnp.dot(wk[...], normed[...], preferred_element_type=jnp.float32)
    k_out[...] = extended(k_t, heads).astype(jnp.bfloat16)
    v_t = jnp.dot(wv[...], normed[...], preferred_element_type=jnp.float32)
    v_out[...] = v_t.astype(jnp.bfloat16)
    hidden_out[...] = hid[...]
    for copy in copies:
        copy.wait_send()
    for copy in q_copies:
        copy.wait()
    qall_out[...] = qall[...]


def pages_kernel(
    heads, nodes, shifts, starts, owner_ref, qall_ref, states_ref, norms_ref,
    first_ref, second_ref, scale_ref, out_ref, total,
):
    step = pl.program_id(0)
    window = first_ref.shape[2]
    value_width = states_ref.shape[1]
    span = heads * nodes

    @pl.when(step == 0)
    def clear():
        total[...] = jnp.zeros_like(total)

    cuts = [(lo, min(lo + 384, window)) for lo in range(0, window, 384)]
    for i in range(len(shifts)):
        owner = owner_ref[step * len(shifts) + i]
        rows = qall_ref[pl.ds(pl.multiple_of(owner * nodes, 16), nodes), :]
        num = jnp.zeros((span, value_width), jnp.float32)
        weigh = jnp.zeros((nodes, 128), jnp.float32)
        for lo, hi in cuts:
            a = jnp.dot(rows, first_ref[i, :, lo:hi], preferred_element_type=jnp.float32)
            b = jnp.dot(rows, second_ref[i, :, lo:hi], preferred_element_type=jnp.float32)
            phi = a * b * scale_ref[i, :, lo:hi]
            weighted = phi * norms_ref[0, i : i + 1, lo:hi]
            for at in range(0, hi - lo, 128):
                part = weighted[:, at : min(at + 128, hi - lo)]
                if part.shape[1] < 128:
                    part = jnp.concatenate(
                        [part, jnp.zeros((nodes, 128 - part.shape[1]), jnp.float32)], axis=1
                    )
                weigh += part
            head_of = lax.broadcasted_iota(jnp.int32, phi.shape, 1) % heads
            masked = jnp.concatenate(
                [jnp.where(head_of == h, phi, 0.0).astype(jnp.bfloat16) for h in range(heads)], axis=0
            )
            num += jnp.dot(
                masked, states_ref[starts[i] + lo : starts[i] + hi, :], preferred_element_type=jnp.float32
            )
        lane_head = lax.broadcasted_iota(jnp.int32, weigh.shape, 1) % heads
        den = jnp.concatenate(
            [
                jnp.sum(jnp.where(lane_head == h, weigh, 0.0), axis=1, keepdims=True)
                for h in range(heads)
            ],
            axis=0,
        )
        at = pl.ds(pl.multiple_of(owner * span, 16), span)
        total[at, 0:value_width] += num
        total[at, value_width : value_width + 1] += den

    @pl.when(step == pl.num_programs(0) - 1)
    def finish():
        out_ref[...] = total[...].astype(jnp.bfloat16)


def layer_kernel(
    heads, feat_width, value_width, requests,
    pref_any, hidden_ref, q_ref, k_ref, v_ref, parent_ref, chosen_ref, gain_ref, first_ref, second_ref,
    wout_any, wgate_any, wup_any, wdown_any,
    out_ref, states_out, norms_out,
    prefs, wout, wgate, wup, wdown, hid, stacked, sums, parts, gathered, blocks, kept, arrived,
    w_sem, own_sem, ps_sem, pr_sem, as_sem, ar_sem, gs_sem, gr_sem, ms_sem, mr_sem,
):
    me_row, me_col = lax.axis_index("row"), lax.axis_index("col")
    row_count = lax.axis_size("row")
    tokens, width = hid.shape
    nodes = tokens // requests
    span = requests * heads * nodes
    unit = heads * feat_width
    loads = [
        pltpu.make_async_copy(src, dst, w_sem.at[i])
        for i, (src, dst) in enumerate(
            ((wout_any, wout), (wgate_any, wgate), (wup_any, wup), (wdown_any, wdown))
        )
    ]
    for load in loads:
        load.start()
    greet()
    block_of = lambda home: pref_any.at[pl.ds(pl.multiple_of(home * span, 16), span)]
    pref_copies = push("col", block_of, prefs.at[me_col], ps_sem, pr_sem)
    own = pltpu.make_async_copy(block_of(me_col), prefs.at[me_col], own_sem)
    own.start()

    row_ids = lax.broadcasted_iota(jnp.int32, (tokens, tokens), 0)
    lane_ids = lax.broadcasted_iota(jnp.int32, (tokens, tokens), 1)
    linked = jnp.logical_or(parent_ref[...] == lane_ids, row_ids == lane_ids)
    reached = jnp.where(linked, 1.0, 0.0)
    for repeat in range(max(1, (nodes - 1).bit_length())):
        low = reached.astype(jnp.bfloat16)
        reached = jnp.minimum(jnp.dot(low, low, preferred_element_type=jnp.float32), 1.0)

    for j in range(width // 128):
        block = hidden_ref[128 * j : 128 * j + 128, :].astype(jnp.float32)
        hid[:, 128 * j : 128 * j + 128] = jnp.transpose(block)

    tree_num, tree_den = [], []
    q = q_ref[...]
    q_lane = lax.broadcasted_iota(jnp.int32, q.shape, 1)
    for h in range(heads):
        mine = jnp.logical_and(q_lane >= h * feat_width, q_lane < (h + 1) * feat_width)
        q_head = jnp.where(mine, q.astype(jnp.float32), 0.0).astype(jnp.bfloat16)
        scaled = jnp.dot(q_head, k_ref[...], preferred_element_type=jnp.float32) / math.sqrt(feat_width)
        kernel = (1.0 + scaled + 0.5 * scaled * scaled) * reached
        tree_den.append(jnp.sum(kernel, axis=1, keepdims=True))
        tree_num.append(
            lax.dot_general(
                kernel.astype(jnp.bfloat16),
                v_ref[h * value_width : (h + 1) * value_width, :],
                (((1,), (1,)), ((), ())),
                preferred_element_type=jnp.float32,
            )
        )

    path = jnp.dot(chosen_ref[...], reached.astype(jnp.bfloat16), preferred_element_type=jnp.float32)
    a = jnp.dot(first_ref[...], k_ref[...], preferred_element_type=jnp.float32)
    b = jnp.dot(second_ref[...], k_ref[...], preferred_element_type=jnp.float32)
    t = lax.broadcasted_iota(jnp.int32, a.shape, 0)
    scale = jnp.where(
        t < heads,
        1.0,
        jnp.where(t < heads * (1 + feat_width), feat_width ** (-0.25), (2.0 * feat_width) ** (-0.5)),
    )
    phi = a * b * scale
    high = phi.astype(jnp.bfloat16)
    rest = (phi - high.astype(jnp.float32)).astype(jnp.bfloat16)
    across = (((1,), (1,)), ((), ()))
    path_low = path.astype(jnp.bfloat16)
    norms_out[...] = lax.dot_general(
        path_low, high, across, preferred_element_type=jnp.float32
    ) + lax.dot_general(path_low, rest, across, preferred_element_type=jnp.float32)
    for h in range(heads):
        stacked[h * tokens : (h + 1) * tokens, :] = jnp.transpose(
            v_ref[h * value_width : (h + 1) * value_width, :].astype(jnp.float32)
        ).astype(jnp.bfloat16)
    count = states_out.shape[0] // requests
    high_full = high.astype(jnp.float32)
    for r in range(requests):
        weighted = high_full * path[r : r + 1, :]
        wide = jnp.concatenate(
            [jnp.where(t % heads == h, weighted, 0.0).astype(jnp.bfloat16) for h in range(heads)], axis=1
        )
        page = jnp.dot(wide, stacked[...], preferred_element_type=jnp.float32)
        states_out[r * count : (r + 1) * count, :] = page[0:count, :].astype(jnp.bfloat16)

    own.wait()
    for copy in pref_copies:
        copy.wait()
    pref = prefs[0].astype(jnp.float32)
    for s in range(1, prefs.shape[0]):
        pref += prefs[s].astype(jnp.float32)
    loads[0].wait()
    partial = jnp.zeros((tokens, width), jnp.float32)
    for h in range(heads):
        rows = jnp.concatenate(
            [pref[(r * heads + h) * nodes : (r * heads + h + 1) * nodes, :] for r in range(requests)], axis=0
        )
        num = rows[:, 0:value_width] + tree_num[h]
        den = rows[:, value_width : value_width + 1] + tree_den[h]
        mixed = (num / den).astype(jnp.bfloat16)
        partial += jnp.dot(
            mixed, wout[h * value_width : (h + 1) * value_width, :], preferred_element_type=jnp.float32
        )
    sums[...] = partial.astype(jnp.bfloat16)

    share = tokens // row_count
    rows_of = lambda row: pl.ds(pl.multiple_of(row * share, 16), share)
    copies = push("row", lambda row: sums.at[rows_of(row)], parts.at[me_row], as_sem, ar_sem)
    parts[me_row] = sums[rows_of(me_row), :]
    for copy in copies:
        copy.wait()
    attn = parts[0].astype(jnp.float32)
    for g in range(1, row_count):
        attn += parts[g].astype(jnp.float32)
    gathered[rows_of(me_row), :] = attn.astype(jnp.bfloat16)
    mine = gathered.at[rows_of(me_row)]
    copies = push("row", lambda row: mine, mine, gs_sem, gr_sem)
    for copy in copies:
        copy.wait()

    residual = hid[...] + gathered[...].astype(jnp.float32)
    feature_share = width // row_count
    for g in range(row_count):
        kept[g] = residual[:, g * feature_share : (g + 1) * feature_share]
    inverse = lax.rsqrt(jnp.sum(residual * residual, axis=1, keepdims=True) / width + epsilon)
    normed = (residual * inverse * gain_ref[...]).astype(jnp.bfloat16)
    loads[1].wait()
    gate = jnp.dot(normed, wgate[...], preferred_element_type=jnp.float32)
    loads[2].wait()
    up = jnp.dot(normed, wup[...], preferred_element_type=jnp.float32)
    active = (gate / (1.0 + jnp.exp(-gate)) * up).astype(jnp.bfloat16)
    loads[3].wait()
    mlp = jnp.dot(active, wdown[...], preferred_element_type=jnp.float32)
    for g in range(row_count):
        blocks[g] = mlp[:, g * feature_share : (g + 1) * feature_share].astype(jnp.bfloat16)
    copies = push("row", lambda row: blocks.at[row], arrived.at[me_row], ms_sem, mr_sem)
    arrived[me_row] = blocks[me_row]
    for copy in copies:
        copy.wait()
    final = kept[me_row]
    for g in range(row_count):
        final += arrived[g].astype(jnp.float32)
    out_ref[...] = final.astype(jnp.bfloat16)


def kernel_local(
    hidden_in, attn_gain, mlp_gain, w_query, w_key, w_value, w_out, w_gate, w_up, w_down,
    page_states, page_norms, page_home, page_request, parents, accepted,
):
    slots, heads, features, value_width = page_states.shape
    feat_width = w_query.shape[1] // heads
    requests, nodes = parents.shape
    tokens, share = hidden_in.shape
    width, hidden_units = w_gate.shape
    rows, cols = lax.axis_size("row"), lax.axis_size("col")
    bf16, f32 = jnp.bfloat16, jnp.float32
    vmem = pl.BlockSpec(memory_space=pltpu.VMEM)
    hbm = pl.BlockSpec(memory_space=pl.ANY)
    dma = pltpu.SemaphoreType.DMA
    unit = heads * feat_width
    limit = 56 * 1024 * 1024

    hidden_t, q_own, q_all, k_t, v_t = pl.pallas_call(
        functools.partial(project_kernel, heads),
        out_shape=(
            jax.ShapeDtypeStruct((width, tokens), bf16),
            jax.ShapeDtypeStruct((tokens, 128), bf16),
            jax.ShapeDtypeStruct((cols * tokens, 128), bf16),
            jax.ShapeDtypeStruct((128, tokens), bf16),
            jax.ShapeDtypeStruct((heads * value_width, tokens), bf16),
        ),
        in_specs=[vmem, vmem, hbm, hbm, hbm],
        out_specs=(vmem,) * 5,
        scratch_shapes=[
            pltpu.VMEM((unit, width), bf16),
            pltpu.VMEM((unit, width), bf16),
            pltpu.VMEM((heads * value_width, width), bf16),
            pltpu.VMEM((width, tokens), bf16),
            pltpu.VMEM((width, tokens), bf16),
            pltpu.VMEM((tokens, 128), bf16),
            pltpu.VMEM((cols * tokens, 128), bf16),
            dma((3,)),
            dma((rows - 1,)),
            dma((rows - 1,)),
            dma((cols - 1,)),
            dma((cols - 1,)),
        ],
        compiler_params=pltpu.CompilerParams(
            collective_id=0, has_side_effects=True, vmem_limit_bytes=limit
        ),
        name="project",
    )(hidden_in.T, attn_gain.reshape(width // 128, 128), w_query.T, w_key.T, w_value.T)

    count = heads * features
    group = 16 // math.gcd(count, 16)
    shifts = [(count * i) % 16 for i in range(group)]
    starts = [count * i - shifts[i] for i in range(group)]
    window = -(-(count + max(shifts)) // 16) * 16
    first, second, scale = expansion(heads, feat_width, shifts, window)
    state_rows = jnp.transpose(page_states, (0, 2, 1, 3)).reshape(slots * count, value_width)
    norm_rows = jnp.transpose(page_norms, (0, 2, 1)).reshape(slots // group, group, count)
    norm_rows = jnp.stack(
        [jnp.pad(norm_rows[:, i], ((0, 0), (s, window - count - s))) for i, s in enumerate(shifts)], axis=1
    )
    owner = (page_home[:, 0] * requests + page_request).astype(jnp.int32)
    total_rows = cols * requests * heads * nodes
    whole = lambda *shape: pl.BlockSpec(shape, lambda s, o: (0,) * len(shape))
    pref = pl.pallas_call(
        functools.partial(pages_kernel, heads, nodes, shifts, starts),
        out_shape=jax.ShapeDtypeStruct((total_rows, 128), bf16),
        grid_spec=pltpu.PrefetchScalarGridSpec(
            num_scalar_prefetch=1,
            grid=(slots // group,),
            in_specs=[
                whole(cols * tokens, 128),
                pl.BlockSpec((group * count, value_width), lambda s, o: (s, 0)),
                pl.BlockSpec((1, group, window), lambda s, o: (s, 0, 0)),
                whole(group, 128, window),
                whole(group, 128, window),
                whole(group, 1, window),
            ],
            out_specs=whole(total_rows, 128),
            scratch_shapes=[pltpu.VMEM((total_rows, 128), f32)],
        ),
        compiler_params=pltpu.CompilerParams(vmem_limit_bytes=limit),
        name="pages",
    )(owner, q_all, state_rows, norm_rows, jnp.asarray(first, bf16), jnp.asarray(second, bf16), jnp.asarray(scale))

    parent_rows = (parents + nodes * jnp.arange(requests, dtype=jnp.int32)[:, None]).reshape(tokens, 1)
    accepted_rows = accepted + nodes * jnp.arange(requests, dtype=jnp.int32)
    chosen = jnp.arange(tokens, dtype=jnp.int32)[None, :] == accepted_rows[:, None]
    chosen = jnp.pad(chosen.astype(bf16), ((0, 16 - requests), (0, 0)))
    first_t = jnp.asarray(first[0].T, bf16)
    second_t = jnp.asarray(second[0].T, bf16)
    span = requests * heads * nodes
    token_share = tokens // rows
    hidden_out, state_out, norm_out = pl.pallas_call(
        functools.partial(layer_kernel, heads, feat_width, value_width, requests),
        out_shape=(
            jax.ShapeDtypeStruct((tokens, share), bf16),
            jax.ShapeDtypeStruct((requests * count, value_width), bf16),
            jax.ShapeDtypeStruct((16, window), f32),
        ),
        in_specs=[hbm] + [vmem] * 9 + [hbm] * 4,
        out_specs=(vmem,) * 3,
        scratch_shapes=[
            pltpu.VMEM((cols, span, 128), bf16),
            pltpu.VMEM(w_out.shape, bf16),
            pltpu.VMEM(w_gate.shape, bf16),
            pltpu.VMEM(w_up.shape, bf16),
            pltpu.VMEM(w_down.shape, bf16),
            pltpu.VMEM((tokens, width), f32),
            pltpu.VMEM((heads * tokens, value_width), bf16),
            pltpu.VMEM((tokens, width), bf16),
            pltpu.VMEM((rows, token_share, width), bf16),
            pltpu.VMEM((tokens, width), bf16),
            pltpu.VMEM((rows, tokens, share), bf16),
            pltpu.VMEM((rows, tokens, share), f32),
            pltpu.VMEM((rows, tokens, share), bf16),
            dma((4,)),
            dma,
            dma((cols - 1,)),
            dma((cols - 1,)),
        ]
        + [dma((rows - 1,))] * 6,
        compiler_params=pltpu.CompilerParams(
            collective_id=1, has_side_effects=True, vmem_limit_bytes=limit
        ),
        name="layer",
    )(
        pref, hidden_t, q_own, k_t, v_t, parent_rows, chosen, mlp_gain.reshape(1, width),
        first_t, second_t, w_out, w_gate, w_up, w_down,
    )
    new_states = jnp.transpose(state_out.reshape(requests, features, heads, value_width), (0, 2, 1, 3))
    new_norms = jnp.transpose(norm_out[:requests, :count].reshape(requests, features, heads), (0, 2, 1))
    return (hidden_out, new_states, new_norms)


def kernels_fit(*arrays):
    hidden_in, w_query, page_states, parents = arrays[0], arrays[3], arrays[10], arrays[14]
    slots, heads, features, value_width = page_states.shape
    tokens, rows = hidden_in.shape[0], lax.axis_size("row")
    group = 16 // math.gcd(heads * features, 16)
    return (
        tokens == 128
        and tokens % (16 * rows) == 0
        and hidden_in.shape[1] % 16 == 0
        and 128 % heads == 0
        and (group == 1 or 16 % heads == 0)
        and w_query.shape[1] + heads <= 128
        and value_width < 128
        and value_width % 16 == 0
        and slots % group == 0
        and parents.shape[0] <= 16
    )


def on_device(*arrays):
    return kernel_local(*arrays) if kernels_fit(*arrays) else local(*arrays)


def solution(mesh):
    return jax.shard_map(
        on_device,
        mesh=mesh,
        in_specs=(
            P("col", "row"),
            P(),
            P(),
            P(None, "row"),
            P(None, "row"),
            P(None, "row"),
            P("row", None),
            P(None, "row"),
            P(None, "row"),
            P("row", None),
            P("col", "row", None, None),
            P("col", "row", None),
            P("col", None),
            P("col"),
            P("col", None),
            P("col"),
        ),
        out_specs=(P("col", "row"), P("col", "row", None, None), P("col", "row", None)),
        check_vma=False,
    )
```

```python
import functools
import math

import jax
import jax.numpy as jnp
import numpy as np
from jax import lax
from jax.experimental import pallas as pl
from jax.experimental.pallas import tpu as pltpu
from jax.sharding import PartitionSpec as P

epsilon = 1e-05


def feature_map(vectors):
    width_in = vectors.shape[-1]
    linear = vectors * width_in ** (-0.25)
    square = vectors[..., :, None] * vectors[..., None, :] * (2.0 * width_in) ** (-0.5)
    square = square.reshape(vectors.shape[:-1] + (width_in * width_in,))
    leading = jnp.ones(vectors.shape[:-1] + (1,), vectors.dtype)
    return jnp.concatenate([leading, linear, square], axis=-1)


def rms_norm(hidden, gain):
    mean_square = jnp.mean(hidden * hidden, axis=-1, keepdims=True)
    return hidden * lax.rsqrt(mean_square + epsilon) * gain


def ancestors(parents):
    nodes = parents.shape[-1]
    node_ids = jnp.arange(nodes, dtype=jnp.int32)
    linked = (parents[..., :, None] == node_ids[None, :]) | (node_ids[:, None] == node_ids[None, :])
    reached = linked.astype(jnp.float32)
    for repeat in range(max(1, (nodes - 1).bit_length())):
        reached = jnp.minimum(
            jnp.einsum("rij,rjk->rik", reached, reached, precision=lax.Precision.HIGHEST), 1.0
        )
    return reached


def pack_slots(homes, requests, col_count, capacity):
    slot_count = homes.shape[0]
    slot_ids = jnp.arange(slot_count, dtype=jnp.int32)
    same_home = (homes[:, None] == homes[None, :]) & (slot_ids[None, :] < slot_ids[:, None])
    ranks = jnp.sum(same_home.astype(jnp.int32), axis=1)
    places = homes * capacity + ranks
    targets = jnp.arange(col_count * capacity, dtype=jnp.int32)
    packer = (targets[:, None] == places[None, :]).astype(jnp.float32)
    labels = (
        jnp.dot(packer, (requests + 1).astype(jnp.float32), precision=lax.Precision.HIGHEST) - 1.0
    )
    return (packer, labels)


def local(
    hidden_in,
    attn_gain,
    mlp_gain,
    w_query,
    w_key,
    w_value,
    w_out,
    w_gate,
    w_up,
    w_down,
    page_states,
    page_norms,
    page_home,
    page_request,
    parents,
    accepted,
):
    highest = lax.Precision.HIGHEST
    local_heads = page_states.shape[1]
    feat_width = w_query.shape[1] // local_heads
    value_width = w_value.shape[1] // local_heads
    req_local = parents.shape[0]
    nodes = parents.shape[1]
    tok_local = hidden_in.shape[0]
    slot_count = page_states.shape[0]
    col_count = lax.axis_size("col")
    row_count = lax.axis_size("row")
    capacity = max(2, 2 * slot_count // col_count)
    row_index = lax.axis_index("row")
    gathered = lax.all_gather(hidden_in, "row", axis=1, tiled=True)
    hidden = gathered.astype(jnp.float32)
    normed = rms_norm(hidden, attn_gain).astype(jnp.bfloat16)
    queries = jnp.dot(normed, w_query, preferred_element_type=jnp.float32).astype(jnp.bfloat16)
    key_rows = jnp.dot(normed, w_key, preferred_element_type=jnp.float32).astype(jnp.bfloat16)
    values = jnp.dot(normed, w_value, preferred_element_type=jnp.float32).astype(jnp.bfloat16)
    query_heads = queries.reshape(req_local, nodes, local_heads, feat_width)
    key_heads = key_rows.reshape(req_local, nodes, local_heads, feat_width)
    value_heads = values.reshape(req_local, nodes, local_heads, value_width)
    reached = ancestors(parents)
    scaled = jnp.einsum(
        "rihf,rjhf->rhij", query_heads, key_heads, preferred_element_type=jnp.float32
    ) / math.sqrt(feat_width)
    kernel = (1.0 + scaled + 0.5 * scaled * scaled) * reached[:, None, :, :]
    tree_den = jnp.transpose(jnp.sum(kernel, axis=-1), (0, 2, 1))
    tree_num = jnp.einsum(
        "rhij,rjhd->rihd",
        kernel.astype(jnp.bfloat16),
        value_heads,
        preferred_element_type=jnp.float32,
    )
    homes = page_home[:, 0]
    packer, packed_ids = pack_slots(homes, page_request, col_count, capacity)
    request_ids = jnp.arange(req_local, dtype=jnp.float32)
    sent_states = jnp.einsum(
        "ps,shfd->phfd",
        packer.astype(jnp.bfloat16),
        page_states,
        preferred_element_type=jnp.float32,
    ).astype(jnp.bfloat16)
    sent_norms = jnp.einsum("ps,shf->phf", packer, page_norms, precision=highest)
    got_states = lax.all_to_all(sent_states, "col", split_axis=0, concat_axis=0, tiled=True)
    got_norms, got_ids = (
        lax.all_to_all(
            sent_norms.astype(jnp.bfloat16), "col", split_axis=0, concat_axis=0, tiled=True
        ).astype(sent_norms.dtype),
        lax.all_to_all(
            packed_ids.astype(jnp.bfloat16), "col", split_axis=0, concat_axis=0, tiled=True
        ).astype(packed_ids.dtype),
    )
    unpack = (got_ids[None, :] == request_ids[:, None]).astype(jnp.float32)
    phi_query = feature_map(query_heads.astype(jnp.float32))
    phi_select = jnp.einsum(
        "rp,rnhf->pnhf",
        unpack.astype(jnp.bfloat16),
        phi_query.astype(jnp.bfloat16),
        preferred_element_type=jnp.float32,
    ).astype(jnp.bfloat16)
    phi_full = jnp.einsum("rp,rnhf->pnhf", unpack, phi_query, precision=highest)
    slot_num = jnp.einsum(
        "pnhf,phfd->pnhd", phi_select, got_states, preferred_element_type=jnp.float32
    )
    slot_den = jnp.einsum("pnhf,phf->pnh", phi_full, got_norms, precision=highest)
    pref_num = jnp.einsum("rp,pnhd->rnhd", unpack, slot_num, precision=highest)
    pref_den = jnp.einsum("rp,pnh->rnh", unpack, slot_den, precision=highest)
    mixed = ((pref_num + tree_num) / (pref_den + tree_den)[..., None]).astype(jnp.bfloat16)
    mixed = mixed.reshape(tok_local, local_heads * value_width)
    partial_value = jnp.dot(mixed, w_out, preferred_element_type=jnp.float32)
    feature_count = partial_value.shape[1]
    share = feature_count // row_count
    attn_all = lax.psum(partial_value.astype(jnp.bfloat16), "row").astype(jnp.float32)
    residual_all = hidden + attn_all
    normed_mlp = rms_norm(residual_all, mlp_gain).astype(jnp.bfloat16)
    residual = lax.dynamic_slice_in_dim(residual_all, row_index * share, share, 1)
    gate_proj = jnp.dot(normed_mlp, w_gate, preferred_element_type=jnp.float32)
    up_proj = jnp.dot(normed_mlp, w_up, preferred_element_type=jnp.float32)
    activated = (jax.nn.silu(gate_proj) * up_proj).astype(jnp.bfloat16)
    mlp_share = lax.psum_scatter(
        jnp.einsum("fd,tf->dt", w_down, activated, preferred_element_type=jnp.float32).astype(
            jnp.bfloat16
        ),
        "row",
        scatter_dimension=0,
        tiled=True,
    ).astype(jnp.float32)
    hidden_out = (residual + jnp.transpose(mlp_share)).astype(jnp.bfloat16)
    node_ids = jnp.arange(nodes, dtype=jnp.int32)
    chosen = (node_ids[None, :] == accepted[:, None]).astype(jnp.float32)
    path_mask = jnp.einsum("ri,rij->rj", chosen, reached, precision=highest)
    phi_key = feature_map(key_heads.astype(jnp.float32))
    new_norms = jnp.einsum("rj,rjhf->rhf", path_mask, phi_key, precision=highest)
    weighted = phi_key.astype(jnp.bfloat16) * path_mask.astype(jnp.bfloat16)[:, :, None, None]
    new_states = jnp.einsum(
        "rjhf,rjhd->rhfd", weighted, value_heads, preferred_element_type=jnp.float32
    ).astype(jnp.bfloat16)
    return (hidden_out, new_states, new_norms)

MESH_KEYS = ("row", "col")


def picks(heads, feat_width, order, length):
    unit = heads * feat_width
    first = np.zeros((length, 128), np.float32)
    second = np.zeros((length, 128), np.float32)
    for h in range(heads):
        for f in range(1 + feat_width + feat_width * feat_width):
            if f == 0:
                a, b = unit + h, unit + h
            elif f <= feat_width:
                a, b = h * feat_width + f - 1, unit + h
            else:
                i, j = divmod(f - 1 - feat_width, feat_width)
                a, b = h * feat_width + i, h * feat_width + j
            first[order(f, h), a] = 1.0
            second[order(f, h), b] = 1.0
    return first, second


def feature_scale(feature, feat_width):
    square = (2.0 * feat_width) ** (-0.5)
    linear = feat_width ** (-0.25)
    return jnp.where(feature == 0, 1.0, jnp.where(feature <= feat_width, linear, square))


def peers_of(axis):
    size, me = lax.axis_size(axis), lax.axis_index(axis)
    return [lax.rem(me + step, size) for step in range(1, size)]


def greet():
    barrier = pltpu.get_barrier_semaphore()
    count = 0
    for axis in MESH_KEYS:
        for peer in peers_of(axis):
            pl.semaphore_signal(
                barrier, inc=1, device_id={axis: peer}, device_id_type=pl.DeviceIdType.MESH
            )
            count += 1
    pl.semaphore_wait(barrier, count)


def push(axis, peers, source_of, target, send_sem, recv_sem):
    copies = []
    for step, peer in enumerate(peers):
        copy = pltpu.make_async_remote_copy(
            src_ref=source_of(step, peer),
            dst_ref=target,
            send_sem=send_sem.at[step],
            recv_sem=recv_sem.at[step],
            device_id={axis: peer},
            device_id_type=pl.DeviceIdType.MESH,
        )
        copy.start()
        copies.append(copy)
    return copies


def extended(rows_t, heads):
    unit, tokens = rows_t.shape
    ids = lax.broadcasted_iota(jnp.int32, (128 - unit, tokens), 0)
    ones = jnp.where(ids < heads, 1.0, 0.0).astype(jnp.bfloat16)
    return jnp.concatenate([rows_t, ones], axis=0)


def dot(a, b, contract=(1, 0)):
    return lax.dot_general(
        a, b, (((contract[0],), (contract[1],)), ((), ())), preferred_element_type=jnp.float32
    )


def layer_kernel(
    heads, feat_width, features, value_width, requests, capacity,
    plan_ref, hidden_ref, gain_ref, mlp_gain_ref, norms_ref, parent_ref, chosen_ref,
    first_ref, second_ref, first_t_ref, second_t_ref, first_h_ref, second_h_ref,
    wq_any, wk_any, wv_any, states_any, wout_any, wgate_any, wup_any, wdown_any,
    out_ref, states_out, norms_out,
    wq, wk, wv, states, wout, wgate, wup, wdown,
    hid_t, normed, q_mine, q_all, k_mine, v_mine, spread, phi_all, nums,
    pair_out, pair_in, chip_out, chip_in,
    hid, stacked, sums, parts, gathered, blocks, kept, arrived,
    w_sem, hs_sem, hr_sem, qs_sem, qr_sem, bs_sem, br_sem, cs_sem, cr_sem,
    as_sem, ar_sem, gs_sem, gr_sem, ms_sem, mr_sem,
):
    bf16, f32 = jnp.bfloat16, jnp.float32
    me_row, me_col = lax.axis_index("row"), lax.axis_index("col")
    row_count, col_count = lax.axis_size("row"), lax.axis_size("col")
    chips = col_count // 2
    me_chip, me_core = me_col // 2, lax.rem(me_col, 2)
    tokens, width = hid.shape
    nodes = tokens // requests
    unit = heads * feat_width
    span = heads * nodes
    count = heads * features
    window = phi_all.shape[2]
    slots = norms_ref.shape[0] // heads
    loads = [
        pltpu.make_async_copy(src, dst, w_sem.at[i])
        for i, (src, dst) in enumerate(
            (
                (wq_any, wq), (wk_any, wk), (wv_any, wv), (states_any, states),
                (wout_any, wout), (wgate_any, wgate), (wup_any, wup), (wdown_any, wdown),
            )
        )
    ]
    for load in loads:
        load.start()
    greet()

    share = hidden_ref.shape[0]
    mine = hid_t.at[pl.ds(pl.multiple_of(me_row * share, 16), share)]
    hidden_copies = push("row", peers_of("row"), lambda i, p: hidden_ref, mine, hs_sem, hr_sem)
    mine[...] = hidden_ref[...]

    gain_t = jnp.transpose(gain_ref[...])
    norms = norms_ref[...]
    f_of = lax.broadcasted_iota(jnp.int32, (features, window), 0)
    t_of = lax.broadcasted_iota(jnp.int32, (features, window), 1)
    expand = jnp.where(t_of // heads == f_of, 1.0, 0.0).astype(bf16)
    top = norms.astype(bf16)
    rest = norms - top.astype(f32)
    middle = rest.astype(bf16)
    low = (rest - middle.astype(f32)).astype(bf16)
    wide = (dot(top, expand) + dot(middle, expand)) + dot(low, expand)
    row_head = lax.broadcasted_iota(jnp.int32, wide.shape, 0) % heads
    lane_head = lax.broadcasted_iota(jnp.int32, wide.shape, 1) % heads
    spread[...] = jnp.where(row_head == lane_head, wide, 0.0)

    row_ids = lax.broadcasted_iota(jnp.int32, (tokens, tokens), 0)
    lane_ids = lax.broadcasted_iota(jnp.int32, (tokens, tokens), 1)
    linked = jnp.logical_or(parent_ref[...] == lane_ids, row_ids == lane_ids)
    reached = jnp.where(linked, 1.0, 0.0)
    for repeat in range(max(1, (nodes - 1).bit_length())):
        reached_low = reached.astype(bf16)
        reached = jnp.minimum(dot(reached_low, reached_low), 1.0)

    for copy in hidden_copies:
        copy.wait_recv()
    total = jnp.zeros((1, tokens), f32)
    for j in range(width // 128):
        x = hid_t[128 * j : 128 * j + 128, :].astype(f32)
        total += jnp.sum(x * x, axis=0, keepdims=True)
    inverse = lax.rsqrt(total / width + epsilon)
    for j in range(width // 128):
        x = hid_t[128 * j : 128 * j + 128, :].astype(f32)
        normed[128 * j : 128 * j + 128, :] = (x * inverse * gain_t[:, j : j + 1]).astype(bf16)
    loads[0].wait()
    q_mine[...] = dot(wq[...], normed[...]).astype(bf16)
    q_copies = push("col", peers_of("col"), lambda i, p: q_mine, q_all.at[me_col], qs_sem, qr_sem)
    q_all[me_col] = q_mine[...]
    loads[1].wait()
    k_mine[...] = dot(wk[...], normed[...]).astype(bf16)
    loads[2].wait()
    v_mine[...] = dot(wv[...], normed[...]).astype(bf16)
    for copy in q_copies:
        copy.wait()

    cuts = [(lo, min(lo + 384, window)) for lo in range(0, window, 384)]
    lane_feature = lax.broadcasted_iota(jnp.int32, (1, window), 1) // heads
    lane_scale = feature_scale(lane_feature, feat_width)

    def features_of(home, carry):
        ext = extended(q_all[home], heads)
        for lo, hi in cuts:
            a = dot(ext, first_ref[:, lo:hi], (0, 0))
            b = dot(ext, second_ref[:, lo:hi], (0, 0))
            phi = a * b * lane_scale[:, lo:hi]
            for r in range(requests):
                phi_all[home * requests + r, :, lo:hi] = phi[r * nodes : (r + 1) * nodes, :]
        return carry

    lax.fori_loop(0, col_count, features_of, 0)

    loads[3].wait()
    group = 16 // math.gcd(count, 16)
    nums[slots] = jnp.zeros((span, 128), f32)

    def slots_of(g, carry):
        norm_rows = spread[pl.ds(pl.multiple_of(g * (group * heads), 8), group * heads), :]
        for i in range(group):
            slot = g * group + i
            shift = (count * i) % 16
            start = count * i - shift
            owner = plan_ref[slot]
            phi = phi_all[owner]
            norm_row = jnp.sum(norm_rows[i * heads : (i + 1) * heads, :], axis=0, keepdims=True)
            weighted = phi * norm_row
            weigh = weighted[:, 0:128]
            for lo in range(128, window, 128):
                weigh += weighted[:, lo : lo + 128]
            lane = lax.broadcasted_iota(jnp.int32, weigh.shape, 1) % heads
            den = [
                jnp.sum(jnp.where(lane == h, weigh, 0.0), axis=1, keepdims=True) for h in range(heads)
            ]
            if shift:
                phi = pltpu.roll(phi, shift, 1)
            head_of = lax.broadcasted_iota(jnp.int32, phi.shape, 1) % heads
            num = jnp.zeros((span, value_width), f32)
            reach = -(-(count + shift) // 16) * 16
            for lo, hi in [(lo, min(lo + 384, reach)) for lo in range(0, reach, 384)]:
                masked = jnp.concatenate(
                    [
                        jnp.where(head_of[:, lo:hi] == h, phi[:, lo:hi], 0.0).astype(bf16)
                        for h in range(heads)
                    ],
                    axis=0,
                )
                rows = pl.ds(pl.multiple_of(g * (group * count) + start + lo, 16), hi - lo)
                num += dot(masked, states[rows, :])
            nums[slot, :, 0:value_width] = num
            nums[slot, :, value_width : value_width + 1] = jnp.concatenate(den, axis=0)
        return carry

    lax.fori_loop(0, slots // group, slots_of, 0)

    def home_sum(home, request):
        acc = jnp.zeros((span, 128), f32)
        for k in range(capacity):
            place = slots + home * capacity + k
            slot = plan_ref[place]
            wanted = jnp.full((span, 128), plan_ref[col_count * capacity + place], jnp.int32)
            acc += jnp.where(wanted == request, nums[slot], 0.0)
        return acc

    for chip in range(chips):
        for r in range(requests):
            pair_out[chip, r * span : (r + 1) * span, :] = home_sum(2 * chip + (1 - me_core), r).astype(bf16)
    pair_copies = push(
        "col", [2 * me_chip + (1 - me_core)], lambda i, p: pair_out, pair_in, bs_sem, br_sem
    )

    k_ext = extended(k_mine[...], heads)
    tree_num, tree_den = [], []
    for h in range(heads):
        at = slice(h * feat_width, (h + 1) * feat_width)
        scaled = dot(q_mine[at, :], k_mine[at, :], (0, 0)) / math.sqrt(feat_width)
        kernel = (1.0 + scaled + 0.5 * scaled * scaled) * reached
        tree_den.append(jnp.sum(kernel, axis=1, keepdims=True))
        tree_num.append(
            dot(kernel.astype(bf16), v_mine[h * value_width : (h + 1) * value_width, :], (1, 1))
        )
    for copy in pair_copies:
        copy.wait()

    def combined(chip, r):
        got = pair_in[chip, r * span : (r + 1) * span, :].astype(f32)
        return home_sum(2 * chip + me_core, r) + got

    chip_peers = [lax.rem(me_chip + step, chips) for step in range(1, chips)]
    chip_copies = []
    for step, chip in enumerate(chip_peers):
        for r in range(requests):
            chip_out[step, r * span : (r + 1) * span, :] = combined(chip, r).astype(bf16)
        copy = pltpu.make_async_remote_copy(
            src_ref=chip_out.at[step],
            dst_ref=chip_in.at[step],
            send_sem=cs_sem.at[step],
            recv_sem=cr_sem.at[step],
            device_id={"col": 2 * chip + me_core},
            device_id_type=pl.DeviceIdType.MESH,
        )
        copy.start()
        chip_copies.append(copy)
    pref = [combined(me_chip, r) for r in range(requests)]

    for j in range(width // 128):
        block = hid_t[128 * j : 128 * j + 128, :].astype(f32)
        hid[:, 128 * j : 128 * j + 128] = jnp.transpose(block)

    path = dot(chosen_ref[...], reached.astype(bf16))
    path_low = path.astype(bf16)
    stride = first_h_ref.shape[0] // heads
    for h in range(heads):
        at = slice(h * stride, (h + 1) * stride)
        feature = lax.broadcasted_iota(jnp.int32, (stride, tokens), 0)
        phi = dot(first_h_ref[at, :], k_ext) * dot(second_h_ref[at, :], k_ext)
        phi = phi * feature_scale(feature, feat_width)
        high = phi.astype(bf16)
        low = (phi - high.astype(f32)).astype(bf16)
        norm = dot(path_low, high, (1, 1)) + dot(path_low, low, (1, 1))
        for r in range(requests):
            norms_out[r * heads + h : r * heads + h + 1, :] = norm[r : r + 1, 0:features]
    phi = dot(first_t_ref[...], k_ext) * dot(second_t_ref[...], k_ext)
    t = lax.broadcasted_iota(jnp.int32, phi.shape, 0)
    high = (phi * feature_scale(t // heads, feat_width)).astype(bf16).astype(f32)
    for h in range(heads):
        values = v_mine[h * value_width : (h + 1) * value_width, :].astype(f32)
        stacked[h * tokens : (h + 1) * tokens, :] = jnp.transpose(values).astype(bf16)
    for r in range(requests):
        weighted = high * path[r : r + 1, :]
        wide = jnp.concatenate(
            [jnp.where(t % heads == h, weighted, 0.0).astype(bf16) for h in range(heads)], axis=1
        )
        page = dot(wide, stacked[...])
        states_out[r * count : (r + 1) * count, :] = page[0:count, :].astype(bf16)

    for copy in chip_copies:
        copy.wait()
    for step in range(chips - 1):
        for r in range(requests):
            pref[r] += chip_in[step, r * span : (r + 1) * span, :].astype(f32)
    loads[4].wait()
    partial = jnp.zeros((tokens, width), f32)
    for h in range(heads):
        rows = jnp.concatenate([pref[r][h * nodes : (h + 1) * nodes, :] for r in range(requests)], axis=0)
        num = rows[:, 0:value_width] + tree_num[h]
        den = rows[:, value_width : value_width + 1] + tree_den[h]
        mixed = (num / den).astype(bf16)
        partial += dot(mixed, wout[h * value_width : (h + 1) * value_width, :])
    sums[...] = partial.astype(bf16)

    token_share = tokens // row_count
    rows_of = lambda row: pl.ds(pl.multiple_of(row * token_share, 16), token_share)
    copies = push(
        "row", peers_of("row"), lambda i, p: sums.at[rows_of(p)], parts.at[me_row], as_sem, ar_sem
    )
    parts[me_row] = sums[rows_of(me_row), :]
    for copy in copies:
        copy.wait()
    attn = parts[0].astype(f32)
    for g in range(1, row_count):
        attn += parts[g].astype(f32)
    gathered[rows_of(me_row), :] = attn.astype(bf16)
    mine = gathered.at[rows_of(me_row)]
    copies = push("row", peers_of("row"), lambda i, p: mine, mine, gs_sem, gr_sem)
    for copy in copies:
        copy.wait()

    residual = hid[...] + gathered[...].astype(f32)
    for g in range(row_count):
        kept[g] = residual[:, g * share : (g + 1) * share]
    inverse = lax.rsqrt(jnp.sum(residual * residual, axis=1, keepdims=True) / width + epsilon)
    normed_mlp = (residual * inverse * mlp_gain_ref[...]).astype(bf16)
    loads[5].wait()
    gate = dot(normed_mlp, wgate[...])
    loads[6].wait()
    up = dot(normed_mlp, wup[...])
    active = (gate / (1.0 + jnp.exp(-gate)) * up).astype(bf16)
    loads[7].wait()
    mlp = dot(active, wdown[...])
    for g in range(row_count):
        blocks[g] = mlp[:, g * share : (g + 1) * share].astype(bf16)
    copies = push("row", peers_of("row"), lambda i, p: blocks.at[p], arrived.at[me_row], ms_sem, mr_sem)
    arrived[me_row] = blocks[me_row]
    for copy in copies:
        copy.wait()
    final = kept[me_row]
    for g in range(row_count):
        final += arrived[g].astype(f32)
    for lo in range(0, share, 128):
        hi = min(lo + 128, share)
        out_ref[lo:hi, :] = jnp.transpose(final[:, lo:hi]).astype(bf16)
    for copy in hidden_copies:
        copy.wait_send()


def kernel_local(
    hidden_in, attn_gain, mlp_gain, w_query, w_key, w_value, w_out, w_gate, w_up, w_down,
    page_states, page_norms, page_home, page_request, parents, accepted,
):
    slots, heads, features, value_width = page_states.shape
    feat_width = w_query.shape[1] // heads
    requests, nodes = parents.shape
    tokens, share = hidden_in.shape
    width = w_gate.shape[0]
    rows, cols = lax.axis_size("row"), lax.axis_size("col")
    capacity = max(2, 2 * slots // cols)
    bf16, f32 = jnp.bfloat16, jnp.float32
    vmem = pl.BlockSpec(memory_space=pltpu.VMEM)
    smem = pl.BlockSpec(memory_space=pltpu.SMEM)
    hbm = pl.BlockSpec(memory_space=pl.ANY)
    dma = pltpu.SemaphoreType.DMA
    unit = heads * feat_width
    span = heads * nodes
    count = heads * features
    window = -(-(count + 16) // 128) * 128

    homes, slot_ids = page_home[:, 0], jnp.arange(slots, dtype=jnp.int32)
    before = (homes[:, None] == homes[None, :]) & (slot_ids[None, :] < slot_ids[:, None])
    places = homes * capacity + jnp.sum(before.astype(jnp.int32), axis=1)
    taken = places[None, :] == jnp.arange(cols * capacity, dtype=jnp.int32)[:, None]
    table = slots + jnp.sum(jnp.where(taken, slot_ids[None, :] - slots, 0), axis=1)
    wanted = jnp.sum(jnp.where(taken, page_request[None, :], 0), axis=1)
    plan = jnp.concatenate([homes * requests + page_request, table, wanted]).astype(jnp.int32)

    state_rows = jnp.transpose(page_states, (0, 2, 1, 3)).reshape(slots * count, value_width)
    parent_rows = (parents + nodes * jnp.arange(requests, dtype=jnp.int32)[:, None]).reshape(tokens, 1)
    accepted_rows = accepted + nodes * jnp.arange(requests, dtype=jnp.int32)
    chosen = jnp.arange(tokens, dtype=jnp.int32)[None, :] == accepted_rows[:, None]
    chosen = jnp.pad(chosen.astype(bf16), ((0, 16 - requests), (0, 0)))
    first, second = picks(heads, feat_width, lambda f, h: f * heads + h, window)
    stride = -(-features // 16) * 16
    first_h, second_h = picks(heads, feat_width, lambda f, h: h * stride + f, heads * stride)
    constants = [jnp.asarray(c, bf16) for c in (first.T, second.T, first, second, first_h, second_h)]
    token_share = tokens // rows
    chips = cols // 2
    hidden_out, state_out, norm_out = pl.pallas_call(
        functools.partial(layer_kernel, heads, feat_width, features, value_width, requests, capacity),
        out_shape=(
            jax.ShapeDtypeStruct((share, tokens), bf16),
            jax.ShapeDtypeStruct((requests * count, value_width), bf16),
            jax.ShapeDtypeStruct((requests * heads, features), f32),
        ),
        in_specs=[smem] + [vmem] * 12 + [hbm] * 8,
        out_specs=(vmem,) * 3,
        scratch_shapes=[
            pltpu.VMEM((unit, width), bf16),
            pltpu.VMEM((unit, width), bf16),
            pltpu.VMEM((heads * value_width, width), bf16),
            pltpu.VMEM(state_rows.shape, bf16),
            pltpu.VMEM(w_out.shape, bf16),
            pltpu.VMEM(w_gate.shape, bf16),
            pltpu.VMEM(w_up.shape, bf16),
            pltpu.VMEM(w_down.shape, bf16),
            pltpu.VMEM((width, tokens), bf16),
            pltpu.VMEM((width, tokens), bf16),
            pltpu.VMEM((unit, tokens), bf16),
            pltpu.VMEM((cols, unit, tokens), bf16),
            pltpu.VMEM((unit, tokens), bf16),
            pltpu.VMEM((heads * value_width, tokens), bf16),
            pltpu.VMEM((slots * heads, window), f32),
            pltpu.VMEM((cols * requests, nodes, window), f32),
            pltpu.VMEM((slots + 1, span, 128), f32),
            pltpu.VMEM((chips, requests * span, 128), bf16),
            pltpu.VMEM((chips, requests * span, 128), bf16),
            pltpu.VMEM((chips - 1, requests * span, 128), bf16),
            pltpu.VMEM((chips - 1, requests * span, 128), bf16),
            pltpu.VMEM((tokens, width), f32),
            pltpu.VMEM((heads * tokens, value_width), bf16),
            pltpu.VMEM((tokens, width), bf16),
            pltpu.VMEM((rows, token_share, width), bf16),
            pltpu.VMEM((tokens, width), bf16),
            pltpu.VMEM((rows, tokens, share), bf16),
            pltpu.VMEM((rows, tokens, share), f32),
            pltpu.VMEM((rows, tokens, share), bf16),
            dma((8,)),
            dma((rows - 1,)),
            dma((rows - 1,)),
            dma((cols - 1,)),
            dma((cols - 1,)),
            dma((1,)),
            dma((1,)),
            dma((chips - 1,)),
            dma((chips - 1,)),
        ]
        + [dma((rows - 1,))] * 6,
        compiler_params=pltpu.CompilerParams(
            collective_id=0, has_side_effects=True, vmem_limit_bytes=58 * 1024 * 1024
        ),
        name="layer",
    )(
        plan, hidden_in.T, attn_gain.reshape(width // 128, 128), mlp_gain.reshape(1, width),
        page_norms.reshape(slots * heads, features), parent_rows, chosen, *constants,
        w_query.T, w_key.T, w_value.T, state_rows, w_out, w_gate, w_up, w_down,
    )
    new_states = jnp.transpose(state_out.reshape(requests, features, heads, value_width), (0, 2, 1, 3))
    return (hidden_out.T, new_states, norm_out.reshape(requests, heads, features))


def kernels_fit(*arrays):
    hidden_in, w_query, page_states, parents = arrays[0], arrays[3], arrays[10], arrays[14]
    slots, heads, features, value_width = page_states.shape
    tokens, rows = hidden_in.shape[0], lax.axis_size("row")
    group = 16 // math.gcd(heads * features, 16)
    return (
        tokens == 128
        and tokens % (16 * rows) == 0
        and hidden_in.shape[1] % 16 == 0
        and 128 % heads == 0
        and (group == 1 or 16 % heads == 0)
        and (group * heads) % 8 == 0
        and w_query.shape[1] + heads <= 128
        and value_width < 128
        and value_width % 16 == 0
        and slots % group == 0
        and parents.shape[0] <= 16
        and lax.axis_size("col") % 2 == 0
        and lax.axis_size("col") > 2
    )


def on_device(*arrays):
    return kernel_local(*arrays) if kernels_fit(*arrays) else local(*arrays)


def solution(mesh):
    return jax.shard_map(
        on_device,
        mesh=mesh,
        in_specs=(
            P("col", "row"),
            P(),
            P(),
            P(None, "row"),
            P(None, "row"),
            P(None, "row"),
            P("row", None),
            P(None, "row"),
            P(None, "row"),
            P("row", None),
            P("col", "row", None, None),
            P("col", "row", None),
            P("col", None),
            P("col"),
            P("col", None),
            P("col"),
        ),
        out_specs=(P("col", "row"), P("col", "row", None, None), P("col", "row", None)),
        check_vma=False,
    )
```

```python
import functools
import math

import jax
import jax.numpy as jnp
import numpy as np
from jax import lax
from jax.experimental import pallas as pl
from jax.experimental.pallas import tpu as pltpu
from jax.sharding import PartitionSpec as P

epsilon = 1e-05


def feature_map(vectors):
    width_in = vectors.shape[-1]
    linear = vectors * width_in ** (-0.25)
    square = vectors[..., :, None] * vectors[..., None, :] * (2.0 * width_in) ** (-0.5)
    square = square.reshape(vectors.shape[:-1] + (width_in * width_in,))
    leading = jnp.ones(vectors.shape[:-1] + (1,), vectors.dtype)
    return jnp.concatenate([leading, linear, square], axis=-1)


def rms_norm(hidden, gain):
    mean_square = jnp.mean(hidden * hidden, axis=-1, keepdims=True)
    return hidden * lax.rsqrt(mean_square + epsilon) * gain


def ancestors(parents):
    nodes = parents.shape[-1]
    node_ids = jnp.arange(nodes, dtype=jnp.int32)
    linked = (parents[..., :, None] == node_ids[None, :]) | (node_ids[:, None] == node_ids[None, :])
    reached = linked.astype(jnp.float32)
    for repeat in range(max(1, (nodes - 1).bit_length())):
        reached = jnp.minimum(
            jnp.einsum("rij,rjk->rik", reached, reached, precision=lax.Precision.HIGHEST), 1.0
        )
    return reached


def pack_slots(homes, requests, col_count, capacity):
    slot_count = homes.shape[0]
    slot_ids = jnp.arange(slot_count, dtype=jnp.int32)
    same_home = (homes[:, None] == homes[None, :]) & (slot_ids[None, :] < slot_ids[:, None])
    ranks = jnp.sum(same_home.astype(jnp.int32), axis=1)
    places = homes * capacity + ranks
    targets = jnp.arange(col_count * capacity, dtype=jnp.int32)
    packer = (targets[:, None] == places[None, :]).astype(jnp.float32)
    labels = (
        jnp.dot(packer, (requests + 1).astype(jnp.float32), precision=lax.Precision.HIGHEST) - 1.0
    )
    return (packer, labels)


def local(
    hidden_in,
    attn_gain,
    mlp_gain,
    w_query,
    w_key,
    w_value,
    w_out,
    w_gate,
    w_up,
    w_down,
    page_states,
    page_norms,
    page_home,
    page_request,
    parents,
    accepted,
):
    highest = lax.Precision.HIGHEST
    local_heads = page_states.shape[1]
    feat_width = w_query.shape[1] // local_heads
    value_width = w_value.shape[1] // local_heads
    req_local = parents.shape[0]
    nodes = parents.shape[1]
    tok_local = hidden_in.shape[0]
    slot_count = page_states.shape[0]
    col_count = lax.axis_size("col")
    row_count = lax.axis_size("row")
    capacity = max(2, 2 * slot_count // col_count)
    row_index = lax.axis_index("row")
    gathered = lax.all_gather(hidden_in, "row", axis=1, tiled=True)
    hidden = gathered.astype(jnp.float32)
    normed = rms_norm(hidden, attn_gain).astype(jnp.bfloat16)
    queries = jnp.dot(normed, w_query, preferred_element_type=jnp.float32).astype(jnp.bfloat16)
    key_rows = jnp.dot(normed, w_key, preferred_element_type=jnp.float32).astype(jnp.bfloat16)
    values = jnp.dot(normed, w_value, preferred_element_type=jnp.float32).astype(jnp.bfloat16)
    query_heads = queries.reshape(req_local, nodes, local_heads, feat_width)
    key_heads = key_rows.reshape(req_local, nodes, local_heads, feat_width)
    value_heads = values.reshape(req_local, nodes, local_heads, value_width)
    reached = ancestors(parents)
    scaled = jnp.einsum(
        "rihf,rjhf->rhij", query_heads, key_heads, preferred_element_type=jnp.float32
    ) / math.sqrt(feat_width)
    kernel = (1.0 + scaled + 0.5 * scaled * scaled) * reached[:, None, :, :]
    tree_den = jnp.transpose(jnp.sum(kernel, axis=-1), (0, 2, 1))
    tree_num = jnp.einsum(
        "rhij,rjhd->rihd",
        kernel.astype(jnp.bfloat16),
        value_heads,
        preferred_element_type=jnp.float32,
    )
    homes = page_home[:, 0]
    packer, packed_ids = pack_slots(homes, page_request, col_count, capacity)
    request_ids = jnp.arange(req_local, dtype=jnp.float32)
    sent_states = jnp.einsum(
        "ps,shfd->phfd",
        packer.astype(jnp.bfloat16),
        page_states,
        preferred_element_type=jnp.float32,
    ).astype(jnp.bfloat16)
    sent_norms = jnp.einsum("ps,shf->phf", packer, page_norms, precision=highest)
    got_states = lax.all_to_all(sent_states, "col", split_axis=0, concat_axis=0, tiled=True)
    got_norms, got_ids = (
        lax.all_to_all(
            sent_norms.astype(jnp.bfloat16), "col", split_axis=0, concat_axis=0, tiled=True
        ).astype(sent_norms.dtype),
        lax.all_to_all(
            packed_ids.astype(jnp.bfloat16), "col", split_axis=0, concat_axis=0, tiled=True
        ).astype(packed_ids.dtype),
    )
    unpack = (got_ids[None, :] == request_ids[:, None]).astype(jnp.float32)
    phi_query = feature_map(query_heads.astype(jnp.float32))
    phi_select = jnp.einsum(
        "rp,rnhf->pnhf",
        unpack.astype(jnp.bfloat16),
        phi_query.astype(jnp.bfloat16),
        preferred_element_type=jnp.float32,
    ).astype(jnp.bfloat16)
    phi_full = jnp.einsum("rp,rnhf->pnhf", unpack, phi_query, precision=highest)
    slot_num = jnp.einsum(
        "pnhf,phfd->pnhd", phi_select, got_states, preferred_element_type=jnp.float32
    )
    slot_den = jnp.einsum("pnhf,phf->pnh", phi_full, got_norms, precision=highest)
    pref_num = jnp.einsum("rp,pnhd->rnhd", unpack, slot_num, precision=highest)
    pref_den = jnp.einsum("rp,pnh->rnh", unpack, slot_den, precision=highest)
    mixed = ((pref_num + tree_num) / (pref_den + tree_den)[..., None]).astype(jnp.bfloat16)
    mixed = mixed.reshape(tok_local, local_heads * value_width)
    partial_value = jnp.dot(mixed, w_out, preferred_element_type=jnp.float32)
    feature_count = partial_value.shape[1]
    share = feature_count // row_count
    attn_all = lax.psum(partial_value.astype(jnp.bfloat16), "row").astype(jnp.float32)
    residual_all = hidden + attn_all
    normed_mlp = rms_norm(residual_all, mlp_gain).astype(jnp.bfloat16)
    residual = lax.dynamic_slice_in_dim(residual_all, row_index * share, share, 1)
    gate_proj = jnp.dot(normed_mlp, w_gate, preferred_element_type=jnp.float32)
    up_proj = jnp.dot(normed_mlp, w_up, preferred_element_type=jnp.float32)
    activated = (jax.nn.silu(gate_proj) * up_proj).astype(jnp.bfloat16)
    mlp_share = lax.psum_scatter(
        jnp.einsum("fd,tf->dt", w_down, activated, preferred_element_type=jnp.float32).astype(
            jnp.bfloat16
        ),
        "row",
        scatter_dimension=0,
        tiled=True,
    ).astype(jnp.float32)
    hidden_out = (residual + jnp.transpose(mlp_share)).astype(jnp.bfloat16)
    node_ids = jnp.arange(nodes, dtype=jnp.int32)
    chosen = (node_ids[None, :] == accepted[:, None]).astype(jnp.float32)
    path_mask = jnp.einsum("ri,rij->rj", chosen, reached, precision=highest)
    phi_key = feature_map(key_heads.astype(jnp.float32))
    new_norms = jnp.einsum("rj,rjhf->rhf", path_mask, phi_key, precision=highest)
    weighted = phi_key.astype(jnp.bfloat16) * path_mask.astype(jnp.bfloat16)[:, :, None, None]
    new_states = jnp.einsum(
        "rjhf,rjhd->rhfd", weighted, value_heads, preferred_element_type=jnp.float32
    ).astype(jnp.bfloat16)
    return (hidden_out, new_states, new_norms)

MESH_KEYS = ("row", "col")


def picks(heads, feat_width, order, length):
    unit = heads * feat_width
    first = np.zeros((length, 128), np.float32)
    second = np.zeros((length, 128), np.float32)
    for h in range(heads):
        for f in range(1 + feat_width + feat_width * feat_width):
            if f == 0:
                a, b = unit + h, unit + h
            elif f <= feat_width:
                a, b = h * feat_width + f - 1, unit + h
            else:
                i, j = divmod(f - 1 - feat_width, feat_width)
                a, b = h * feat_width + i, h * feat_width + j
            first[order(f, h), a] = 1.0
            second[order(f, h), b] = 1.0
    return first, second


def feature_scale(feature, feat_width):
    square = (2.0 * feat_width) ** (-0.5)
    linear = feat_width ** (-0.25)
    return jnp.where(feature == 0, 1.0, jnp.where(feature <= feat_width, linear, square))


def peers_of(axis):
    size, me = lax.axis_size(axis), lax.axis_index(axis)
    return [lax.rem(me + step, size) for step in range(1, size)]


def greet():
    barrier = pltpu.get_barrier_semaphore()
    count = 0
    for axis in MESH_KEYS:
        for peer in peers_of(axis):
            pl.semaphore_signal(
                barrier, inc=1, device_id={axis: peer}, device_id_type=pl.DeviceIdType.MESH
            )
            count += 1
    pl.semaphore_wait(barrier, count)


def push(axis, peers, source_of, target, send_sem, recv_sem, base=0):
    copies = []
    for step, peer in enumerate(peers):
        copy = pltpu.make_async_remote_copy(
            src_ref=source_of(step, peer),
            dst_ref=target,
            send_sem=send_sem.at[base + step],
            recv_sem=recv_sem.at[base + step],
            device_id={axis: peer},
            device_id_type=pl.DeviceIdType.MESH,
        )
        copy.start()
        copies.append(copy)
    return copies


def extended(rows_t, heads):
    unit, tokens = rows_t.shape
    ids = lax.broadcasted_iota(jnp.int32, (128 - unit, tokens), 0)
    ones = jnp.where(ids < heads, 1.0, 0.0).astype(jnp.bfloat16)
    return jnp.concatenate([rows_t, ones], axis=0)


def dot(a, b, contract=(1, 0)):
    return lax.dot_general(
        a, b, (((contract[0],), (contract[1],)), ((), ())), preferred_element_type=jnp.float32
    )


def layer_kernel(
    heads, feat_width, features, value_width, requests, capacity,
    home_ref, request_ref, accepted_ref, hidden_ref, gain_ref, mlp_gain_ref, norms_ref, parent_ref,
    first_any, second_any, first_t_any, second_t_any, first_h_any, second_h_any,
    wq_any, wk_any, wv_any, states_any, wout_any, wgate_any, wup_any, wdown_any,
    out_ref, states_out, norms_out,
    wq, wk, wv, states, wout, wgate, wup, wdown,
    first_ref, second_ref, first_t_ref, second_t_ref, first_h_ref, second_h_ref, table, norms_flat, normed_mlp,
    hid_t, normed, q_mine, q_all, k_mine, v_mine, spread, phi_all, nums,
    pair_out, pair_in, chip_out, chip_in,
    hid, stacked, sums, parts, gathered, blocks, kept, arrived,
    w_sem, hs_sem, hr_sem, qs_sem, qr_sem, bs_sem, br_sem, cs_sem, cr_sem,
    as_sem, ar_sem, gs_sem, gr_sem, ms_sem, mr_sem,
):
    bf16, f32 = jnp.bfloat16, jnp.float32
    me_row, me_col = lax.axis_index("row"), lax.axis_index("col")
    row_count, col_count = lax.axis_size("row"), lax.axis_size("col")
    chips = col_count // 2
    me_chip, me_core = me_col // 2, lax.rem(me_col, 2)
    tokens, width = hid.shape
    nodes = tokens // requests
    unit = heads * feat_width
    span = heads * nodes
    count = heads * features
    window = phi_all.shape[2]
    slots = norms_ref.shape[0]
    loads = [
        pltpu.make_async_copy(src, dst, w_sem.at[i])
        for i, (src, dst) in enumerate(
            (
                (wq_any, wq), (wk_any, wk), (wv_any, wv), (states_any, states),
                (wout_any, wout), (wgate_any, wgate), (wup_any, wup), (wdown_any, wdown),
                (first_any, first_ref), (second_any, second_ref),
                (first_t_any, first_t_ref), (second_t_any, second_t_ref),
                (first_h_any, first_h_ref), (second_h_any, second_h_ref),
            )
        )
    ]
    for i in (0, 1, 2, 8, 9, 3, 10, 11, 12, 13, 4, 5, 6, 7):
        loads[i].start()
    greet()

    share = hidden_ref.shape[0]
    mine = hid_t.at[pl.ds(pl.multiple_of(me_row * share, 16), share)]
    hidden_copies = push("row", peers_of("row"), lambda i, p: hidden_ref, mine, hs_sem, hr_sem)
    mine[...] = hidden_ref[...]

    gain_t = jnp.transpose(gain_ref[...])
    for slot in range(slots):
        norms_flat[slot * heads : (slot + 1) * heads, :] = norms_ref[slot]
    norms = norms_flat[...]
    f_of = lax.broadcasted_iota(jnp.int32, (features, window), 0)
    t_of = lax.broadcasted_iota(jnp.int32, (features, window), 1)
    expand = jnp.where(t_of // heads == f_of, 1.0, 0.0).astype(bf16)
    top = norms.astype(bf16)
    rest = norms - top.astype(f32)
    middle = rest.astype(bf16)
    low = (rest - middle.astype(f32)).astype(bf16)
    wide = (dot(top, expand) + dot(middle, expand)) + dot(low, expand)
    row_head = lax.broadcasted_iota(jnp.int32, wide.shape, 0) % heads
    lane_head = lax.broadcasted_iota(jnp.int32, wide.shape, 1) % heads
    spread[...] = jnp.where(row_head == lane_head, wide, 0.0)

    row_ids = lax.broadcasted_iota(jnp.int32, (tokens, tokens), 0)
    lane_ids = lax.broadcasted_iota(jnp.int32, (tokens, tokens), 1)
    parent_row = jnp.concatenate(
        [parent_ref[r : r + 1, :] + r * nodes for r in range(requests)], axis=1
    )
    linked = jnp.logical_or(parent_row == row_ids, row_ids == lane_ids)
    reached = jnp.where(linked, 1.0, 0.0)
    for repeat in range(max(1, (nodes - 1).bit_length())):
        reached_low = reached.astype(bf16)
        reached = jnp.minimum(dot(reached_low, reached_low), 1.0)
    reached = jnp.transpose(reached)

    homes = [home_ref[slot] for slot in range(slots)]
    places = []
    for slot in range(slots):
        rank = jnp.int32(0)
        for earlier in range(slot):
            rank += (homes[earlier] == homes[slot]).astype(jnp.int32)
        places.append(homes[slot] * capacity + rank)
    for place in range(col_count * capacity):
        found = jnp.int32(slots)
        for slot in range(slots):
            found += (places[slot] == place).astype(jnp.int32) * (slot - slots)
        table[place] = found

    for copy in hidden_copies:
        copy.wait_recv()
    total = jnp.zeros((1, tokens), f32)
    for j in range(width // 128):
        x = hid_t[128 * j : 128 * j + 128, :].astype(f32)
        total += jnp.sum(x * x, axis=0, keepdims=True)
    inverse = lax.rsqrt(total / width + epsilon)
    for j in range(width // 128):
        x = hid_t[128 * j : 128 * j + 128, :].astype(f32)
        normed[128 * j : 128 * j + 128, :] = (x * inverse * gain_t[:, j : j + 1]).astype(bf16)
    loads[0].wait()
    q_mine[...] = dot(wq[...], normed[...]).astype(bf16)
    q_copies = push("col", peers_of("col"), lambda i, p: q_mine, q_all.at[me_col], qs_sem, qr_sem)
    q_all[me_col] = q_mine[...]
    loads[1].wait()
    k_mine[...] = dot(wk[...], normed[...]).astype(bf16)
    loads[2].wait()
    v_mine[...] = dot(wv[...], normed[...]).astype(bf16)
    for copy in q_copies:
        copy.wait()

    loads[8].wait()
    loads[9].wait()
    cuts = [(lo, min(lo + 384, window)) for lo in range(0, window, 384)]
    lane_feature = lax.broadcasted_iota(jnp.int32, (1, window), 1) // heads
    lane_scale = feature_scale(lane_feature, feat_width)

    def features_of(home, carry):
        ext = extended(q_all[home], heads)
        for lo, hi in cuts:
            a = dot(ext, first_ref[:, lo:hi], (0, 0))
            b = dot(ext, second_ref[:, lo:hi], (0, 0))
            phi = a * b * lane_scale[:, lo:hi]
            for r in range(requests):
                phi_all[home * requests + r, :, lo:hi] = phi[r * nodes : (r + 1) * nodes, :]
        return carry

    lax.fori_loop(0, col_count, features_of, 0)

    loads[3].wait()
    group = 16 // math.gcd(count, 16)
    nums[slots] = jnp.zeros((span, 128), f32)

    def slots_of(g, carry):
        norm_rows = spread[pl.ds(pl.multiple_of(g * (group * heads), 8), group * heads), :]
        for i in range(group):
            slot = g * group + i
            shift = (count * i) % 16
            start = count * i - shift
            owner = home_ref[slot] * requests + request_ref[slot]
            phi = phi_all[owner]
            norm_row = jnp.sum(norm_rows[i * heads : (i + 1) * heads, :], axis=0, keepdims=True)
            weighted = phi * norm_row
            weigh = weighted[:, 0:128]
            for lo in range(128, window, 128):
                weigh += weighted[:, lo : lo + 128]
            lane = lax.broadcasted_iota(jnp.int32, weigh.shape, 1) % heads
            den = [
                jnp.sum(jnp.where(lane == h, weigh, 0.0), axis=1, keepdims=True) for h in range(heads)
            ]
            if shift:
                phi = pltpu.roll(phi, shift, 1)
            head_of = lax.broadcasted_iota(jnp.int32, phi.shape, 1) % heads
            num = jnp.zeros((span, value_width), f32)
            reach = -(-(count + shift) // 16) * 16
            for lo, hi in [(lo, min(lo + 384, reach)) for lo in range(0, reach, 384)]:
                masked = jnp.concatenate(
                    [
                        jnp.where(head_of[:, lo:hi] == h, phi[:, lo:hi], 0.0).astype(bf16)
                        for h in range(heads)
                    ],
                    axis=0,
                )
                rows = pl.ds(pl.multiple_of(g * (group * count) + start + lo, 16), hi - lo)
                num += dot(masked, states[rows, :])
            nums[slot, :, 0:value_width] = num
            nums[slot, :, value_width : value_width + 1] = jnp.concatenate(den, axis=0)
        return carry

    lax.fori_loop(0, slots // group, slots_of, 0)

    def home_sum(home, request):
        acc = jnp.zeros((span, 128), f32)
        for k in range(capacity):
            slot = table[home * capacity + k]
            wanted = jnp.full((span, 128), request_ref[jnp.minimum(slot, slots - 1)], jnp.int32)
            acc += jnp.where(wanted == request, nums[slot], 0.0)
        return acc

    for chip in range(chips):
        for r in range(requests):
            pair_out[chip, r * span : (r + 1) * span, :] = home_sum(2 * chip + (1 - me_core), r).astype(bf16)
    pair_copies = push(
        "col", [2 * me_chip + (1 - me_core)], lambda i, p: pair_out, pair_in, bs_sem, br_sem
    )

    k_ext = extended(k_mine[...], heads)
    tree_num, tree_den = [], []
    for h in range(heads):
        at = slice(h * feat_width, (h + 1) * feat_width)
        scaled = dot(q_mine[at, :], k_mine[at, :], (0, 0)) / math.sqrt(feat_width)
        kernel = (1.0 + scaled + 0.5 * scaled * scaled) * reached
        tree_den.append(jnp.sum(kernel, axis=1, keepdims=True))
        tree_num.append(
            dot(kernel.astype(bf16), v_mine[h * value_width : (h + 1) * value_width, :], (1, 1))
        )
    for copy in pair_copies:
        copy.wait()

    def combined(chip, r):
        got = pair_in[chip, r * span : (r + 1) * span, :].astype(f32)
        return home_sum(2 * chip + me_core, r) + got

    chip_peers = [lax.rem(me_chip + step, chips) for step in range(1, chips)]
    chip_copies = []
    for r in range(requests):
        for step, chip in enumerate(chip_peers):
            chip_out[r, step] = combined(chip, r).astype(bf16)
            chip_copies += push(
                "col", [2 * chip + me_core], lambda i, p: chip_out.at[r, step], chip_in.at[r, step],
                cs_sem, cr_sem, r * (chips - 1) + step,
            )
    pref = [combined(me_chip, r) for r in range(requests)]

    for j in range(width // 128):
        block = hid_t[128 * j : 128 * j + 128, :].astype(f32)
        hid[:, 128 * j : 128 * j + 128] = jnp.transpose(block)

    for i in range(10, 14):
        loads[i].wait()
    pick_row = lax.broadcasted_iota(jnp.int32, (16, tokens), 0)
    pick_lane = lax.broadcasted_iota(jnp.int32, (16, tokens), 1)
    chosen = jnp.zeros((16, tokens), f32)
    for r in range(requests):
        hit = jnp.logical_and(pick_row == r, pick_lane == accepted_ref[r] + r * nodes)
        chosen = jnp.where(hit, 1.0, chosen)
    path = dot(chosen.astype(bf16), reached.astype(bf16))
    path_low = path.astype(bf16)
    stride = first_h_ref.shape[0] // heads
    for h in range(heads):
        at = slice(h * stride, (h + 1) * stride)
        feature = lax.broadcasted_iota(jnp.int32, (stride, tokens), 0)
        phi = dot(first_h_ref[at, :], k_ext) * dot(second_h_ref[at, :], k_ext)
        phi = phi * feature_scale(feature, feat_width)
        high = phi.astype(bf16)
        low = (phi - high.astype(f32)).astype(bf16)
        norm = dot(path_low, high, (1, 1)) + dot(path_low, low, (1, 1))
        for r in range(requests):
            norms_out[r, h : h + 1, :] = norm[r : r + 1, 0:features]
    phi = dot(first_t_ref[...], k_ext) * dot(second_t_ref[...], k_ext)
    t = lax.broadcasted_iota(jnp.int32, phi.shape, 0)
    high = (phi * feature_scale(t // heads, feat_width)).astype(bf16).astype(f32)
    for h in range(heads):
        values = v_mine[h * value_width : (h + 1) * value_width, :].astype(f32)
        stacked[h * tokens : (h + 1) * tokens, :] = jnp.transpose(values).astype(bf16)
    for r in range(requests):
        weighted = high * path[r : r + 1, :]
        wide = jnp.concatenate(
            [jnp.where(t % heads == h, weighted, 0.0).astype(bf16) for h in range(heads)], axis=1
        )
        page = dot(wide, stacked[...])
        states_out[r * count : (r + 1) * count, :] = page[0:count, :].astype(bf16)

    token_share = nodes // row_count
    steps = row_count - 1
    row_peers = peers_of("row")
    rows_of = lambda row: pl.ds(pl.multiple_of(row * token_share, 16), token_share)
    loads[4].wait()
    sum_copies = []
    for r in range(requests):
        for step in range(chips - 1):
            chip_copies[r * (chips - 1) + step].wait()
            pref[r] += chip_in[r, step].astype(f32)
        partial = jnp.zeros((nodes, width), f32)
        for h in range(heads):
            rows = pref[r][h * nodes : (h + 1) * nodes, :]
            at = slice(r * nodes, (r + 1) * nodes)
            num = rows[:, 0:value_width] + tree_num[h][at, :]
            den = rows[:, value_width : value_width + 1] + tree_den[h][at, :]
            mixed = (num / den).astype(bf16)
            partial += dot(mixed, wout[h * value_width : (h + 1) * value_width, :])
        sums[r] = partial.astype(bf16)
        sum_copies.append(
            push(
                "row", row_peers, lambda i, p: sums.at[r, rows_of(p)], parts.at[r, me_row],
                as_sem, ar_sem, r * steps,
            )
        )
        parts[r, me_row] = sums[r, rows_of(me_row), :]

    gather_copies = []
    for r in range(requests):
        for copy in sum_copies[r]:
            copy.wait()
        attn = parts[r, 0].astype(f32)
        for g in range(1, row_count):
            attn += parts[r, g].astype(f32)
        gathered[r, rows_of(me_row), :] = attn.astype(bf16)
        mine = gathered.at[r, rows_of(me_row)]
        gather_copies.append(
            push("row", row_peers, lambda i, p: mine, mine, gs_sem, gr_sem, r * steps)
        )

    mlp_copies = []
    for r in range(requests):
        for copy in gather_copies[r]:
            copy.wait()
        residual = hid[r * nodes : (r + 1) * nodes, :] + gathered[r].astype(f32)
        for g in range(row_count):
            kept[r, g] = residual[:, g * share : (g + 1) * share]
        inverse = lax.rsqrt(jnp.sum(residual * residual, axis=1, keepdims=True) / width + epsilon)
        for j in range(width // 128):
            at = slice(128 * j, 128 * j + 128)
            scaled = residual[:, at] * inverse * mlp_gain_ref[j : j + 1, :]
            normed_mlp[r, :, at] = scaled.astype(bf16)
        if r == 0:
            loads[5].wait()
        gate = dot(normed_mlp[r], wgate[...])
        if r == 0:
            loads[6].wait()
        up = dot(normed_mlp[r], wup[...])
        active = (gate / (1.0 + jnp.exp(-gate)) * up).astype(bf16)
        if r == 0:
            loads[7].wait()
        mlp = dot(active, wdown[...])
        for g in range(row_count):
            blocks[r, g] = mlp[:, g * share : (g + 1) * share].astype(bf16)
        mlp_copies.append(
            push(
                "row", row_peers, lambda i, p: blocks.at[r, p], arrived.at[r, me_row],
                ms_sem, mr_sem, r * steps,
            )
        )
        arrived[r, me_row] = blocks[r, me_row]
    finals = []
    for r in range(requests):
        for copy in mlp_copies[r]:
            copy.wait()
        final = kept[r, me_row]
        for g in range(row_count):
            final += arrived[r, g].astype(f32)
        finals.append(final)
    final = jnp.concatenate(finals, axis=0)
    for lo in range(0, share, 128):
        hi = min(lo + 128, share)
        out_ref[lo:hi, :] = jnp.transpose(final[:, lo:hi]).astype(bf16)
    for copy in hidden_copies:
        copy.wait_send()


def kernel_local(
    hidden_in, attn_gain, mlp_gain, w_query, w_key, w_value, w_out, w_gate, w_up, w_down,
    page_states, page_norms, page_home, page_request, parents, accepted,
):
    slots, heads, features, value_width = page_states.shape
    feat_width = w_query.shape[1] // heads
    requests, nodes = parents.shape
    tokens, share = hidden_in.shape
    width = w_gate.shape[0]
    rows, cols = lax.axis_size("row"), lax.axis_size("col")
    capacity = max(2, 2 * slots // cols)
    bf16, f32 = jnp.bfloat16, jnp.float32
    vmem = pl.BlockSpec(memory_space=pltpu.VMEM)
    smem = pl.BlockSpec(memory_space=pltpu.SMEM)
    hbm = pl.BlockSpec(memory_space=pl.ANY)
    dma = pltpu.SemaphoreType.DMA
    unit = heads * feat_width
    span = heads * nodes
    count = heads * features
    window = -(-(count + 16) // 128) * 128

    state_rows = jnp.transpose(page_states, (0, 2, 1, 3)).reshape(slots * count, value_width)
    first, second = picks(heads, feat_width, lambda f, h: f * heads + h, window)
    stride = -(-features // 16) * 16
    first_h, second_h = picks(heads, feat_width, lambda f, h: h * stride + f, heads * stride)
    constants = [jnp.asarray(c, bf16) for c in (first.T, second.T, first, second, first_h, second_h)]
    token_share = nodes // rows
    chips = cols // 2
    hidden_out, state_out, norm_out = pl.pallas_call(
        functools.partial(layer_kernel, heads, feat_width, features, value_width, requests, capacity),
        out_shape=(
            jax.ShapeDtypeStruct((share, tokens), bf16),
            jax.ShapeDtypeStruct((requests * count, value_width), bf16),
            jax.ShapeDtypeStruct((requests, heads, features), f32),
        ),
        in_specs=[smem] * 3 + [vmem] * 5 + [hbm] * 14,
        out_specs=(vmem,) * 3,
        scratch_shapes=[
            pltpu.VMEM((unit, width), bf16),
            pltpu.VMEM((unit, width), bf16),
            pltpu.VMEM((heads * value_width, width), bf16),
            pltpu.VMEM(state_rows.shape, bf16),
            pltpu.VMEM(w_out.shape, bf16),
            pltpu.VMEM(w_gate.shape, bf16),
            pltpu.VMEM(w_up.shape, bf16),
            pltpu.VMEM(w_down.shape, bf16),
        ]
        + [pltpu.VMEM(c.shape, bf16) for c in constants]
        + [
            pltpu.SMEM((cols * capacity,), jnp.int32),
            pltpu.VMEM((slots * heads, features), f32),
            pltpu.VMEM((requests, nodes, width), bf16),
            pltpu.VMEM((width, tokens), bf16),
            pltpu.VMEM((width, tokens), bf16),
            pltpu.VMEM((unit, tokens), bf16),
            pltpu.VMEM((cols, unit, tokens), bf16),
            pltpu.VMEM((unit, tokens), bf16),
            pltpu.VMEM((heads * value_width, tokens), bf16),
            pltpu.VMEM((slots * heads, window), f32),
            pltpu.VMEM((cols * requests, nodes, window), f32),
            pltpu.VMEM((slots + 1, span, 128), f32),
            pltpu.VMEM((chips, requests * span, 128), bf16),
            pltpu.VMEM((chips, requests * span, 128), bf16),
            pltpu.VMEM((requests, chips - 1, span, 128), bf16),
            pltpu.VMEM((requests, chips - 1, span, 128), bf16),
            pltpu.VMEM((tokens, width), f32),
            pltpu.VMEM((heads * tokens, value_width), bf16),
            pltpu.VMEM((requests, nodes, width), bf16),
            pltpu.VMEM((requests, rows, token_share, width), bf16),
            pltpu.VMEM((requests, nodes, width), bf16),
            pltpu.VMEM((requests, rows, nodes, share), bf16),
            pltpu.VMEM((requests, rows, nodes, share), f32),
            pltpu.VMEM((requests, rows, nodes, share), bf16),
            dma((14,)),
            dma((rows - 1,)),
            dma((rows - 1,)),
            dma((cols - 1,)),
            dma((cols - 1,)),
            dma((1,)),
            dma((1,)),
            dma((requests * (chips - 1),)),
            dma((requests * (chips - 1),)),
        ]
        + [dma((requests * (rows - 1),))] * 6,
        compiler_params=pltpu.CompilerParams(
            collective_id=0, has_side_effects=True, vmem_limit_bytes=58 * 1024 * 1024
        ),
        name="layer",
    )(
        page_home[:, 0], page_request, accepted, hidden_in.T, attn_gain.reshape(width // 128, 128),
        mlp_gain.reshape(width // 128, 128), page_norms, parents, *constants,
        w_query.T, w_key.T, w_value.T, state_rows, w_out, w_gate, w_up, w_down,
    )
    new_states = jnp.transpose(state_out.reshape(requests, features, heads, value_width), (0, 2, 1, 3))
    return (hidden_out.T, new_states, norm_out)


def kernels_fit(*arrays):
    hidden_in, w_query, page_states, parents = arrays[0], arrays[3], arrays[10], arrays[14]
    slots, heads, features, value_width = page_states.shape
    tokens, rows = hidden_in.shape[0], lax.axis_size("row")
    group = 16 // math.gcd(heads * features, 16)
    return (
        tokens == 128
        and parents.shape[1] % (16 * rows) == 0
        and hidden_in.shape[1] % 16 == 0
        and 128 % heads == 0
        and (group == 1 or 16 % heads == 0)
        and (group * heads) % 8 == 0
        and w_query.shape[1] + heads <= 128
        and value_width < 128
        and value_width % 16 == 0
        and slots % group == 0
        and parents.shape[0] <= 16
        and lax.axis_size("col") % 2 == 0
        and lax.axis_size("col") > 2
    )


def on_device(*arrays):
    return kernel_local(*arrays) if kernels_fit(*arrays) else local(*arrays)


def solution(mesh):
    return jax.shard_map(
        on_device,
        mesh=mesh,
        in_specs=(
            P("col", "row"),
            P(),
            P(),
            P(None, "row"),
            P(None, "row"),
            P(None, "row"),
            P("row", None),
            P(None, "row"),
            P(None, "row"),
            P("row", None),
            P("col", "row", None, None),
            P("col", "row", None),
            P("col", None),
            P("col"),
            P("col", None),
            P("col"),
        ),
        out_specs=(P("col", "row"), P("col", "row", None, None), P("col", "row", None)),
        check_vma=False,
    )
```

```python
import functools
import math

import jax
import jax.numpy as jnp
import numpy as np
from jax import lax
from jax.experimental import pallas as pl
from jax.experimental.pallas import tpu as pltpu
from jax.sharding import PartitionSpec as P

epsilon = 1e-05


def feature_map(vectors):
    width_in = vectors.shape[-1]
    linear = vectors * width_in ** (-0.25)
    square = vectors[..., :, None] * vectors[..., None, :] * (2.0 * width_in) ** (-0.5)
    square = square.reshape(vectors.shape[:-1] + (width_in * width_in,))
    leading = jnp.ones(vectors.shape[:-1] + (1,), vectors.dtype)
    return jnp.concatenate([leading, linear, square], axis=-1)


def rms_norm(hidden, gain):
    mean_square = jnp.mean(hidden * hidden, axis=-1, keepdims=True)
    return hidden * lax.rsqrt(mean_square + epsilon) * gain


def ancestors(parents):
    nodes = parents.shape[-1]
    node_ids = jnp.arange(nodes, dtype=jnp.int32)
    linked = (parents[..., :, None] == node_ids[None, :]) | (node_ids[:, None] == node_ids[None, :])
    reached = linked.astype(jnp.float32)
    for repeat in range(max(1, (nodes - 1).bit_length())):
        reached = jnp.minimum(
            jnp.einsum("rij,rjk->rik", reached, reached, precision=lax.Precision.HIGHEST), 1.0
        )
    return reached


def pack_slots(homes, requests, col_count, capacity):
    slot_count = homes.shape[0]
    slot_ids = jnp.arange(slot_count, dtype=jnp.int32)
    same_home = (homes[:, None] == homes[None, :]) & (slot_ids[None, :] < slot_ids[:, None])
    ranks = jnp.sum(same_home.astype(jnp.int32), axis=1)
    places = homes * capacity + ranks
    targets = jnp.arange(col_count * capacity, dtype=jnp.int32)
    packer = (targets[:, None] == places[None, :]).astype(jnp.float32)
    labels = (
        jnp.dot(packer, (requests + 1).astype(jnp.float32), precision=lax.Precision.HIGHEST) - 1.0
    )
    return (packer, labels)


def local(
    hidden_in,
    attn_gain,
    mlp_gain,
    w_query,
    w_key,
    w_value,
    w_out,
    w_gate,
    w_up,
    w_down,
    page_states,
    page_norms,
    page_home,
    page_request,
    parents,
    accepted,
):
    highest = lax.Precision.HIGHEST
    local_heads = page_states.shape[1]
    feat_width = w_query.shape[1] // local_heads
    value_width = w_value.shape[1] // local_heads
    req_local = parents.shape[0]
    nodes = parents.shape[1]
    tok_local = hidden_in.shape[0]
    slot_count = page_states.shape[0]
    col_count = lax.axis_size("col")
    row_count = lax.axis_size("row")
    capacity = max(2, 2 * slot_count // col_count)
    row_index = lax.axis_index("row")
    gathered = lax.all_gather(hidden_in, "row", axis=1, tiled=True)
    hidden = gathered.astype(jnp.float32)
    normed = rms_norm(hidden, attn_gain).astype(jnp.bfloat16)
    queries = jnp.dot(normed, w_query, preferred_element_type=jnp.float32).astype(jnp.bfloat16)
    key_rows = jnp.dot(normed, w_key, preferred_element_type=jnp.float32).astype(jnp.bfloat16)
    values = jnp.dot(normed, w_value, preferred_element_type=jnp.float32).astype(jnp.bfloat16)
    query_heads = queries.reshape(req_local, nodes, local_heads, feat_width)
    key_heads = key_rows.reshape(req_local, nodes, local_heads, feat_width)
    value_heads = values.reshape(req_local, nodes, local_heads, value_width)
    reached = ancestors(parents)
    scaled = jnp.einsum(
        "rihf,rjhf->rhij", query_heads, key_heads, preferred_element_type=jnp.float32
    ) / math.sqrt(feat_width)
    kernel = (1.0 + scaled + 0.5 * scaled * scaled) * reached[:, None, :, :]
    tree_den = jnp.transpose(jnp.sum(kernel, axis=-1), (0, 2, 1))
    tree_num = jnp.einsum(
        "rhij,rjhd->rihd",
        kernel.astype(jnp.bfloat16),
        value_heads,
        preferred_element_type=jnp.float32,
    )
    homes = page_home[:, 0]
    packer, packed_ids = pack_slots(homes, page_request, col_count, capacity)
    request_ids = jnp.arange(req_local, dtype=jnp.float32)
    sent_states = jnp.einsum(
        "ps,shfd->phfd",
        packer.astype(jnp.bfloat16),
        page_states,
        preferred_element_type=jnp.float32,
    ).astype(jnp.bfloat16)
    sent_norms = jnp.einsum("ps,shf->phf", packer, page_norms, precision=highest)
    got_states = lax.all_to_all(sent_states, "col", split_axis=0, concat_axis=0, tiled=True)
    got_norms, got_ids = (
        lax.all_to_all(
            sent_norms.astype(jnp.bfloat16), "col", split_axis=0, concat_axis=0, tiled=True
        ).astype(sent_norms.dtype),
        lax.all_to_all(
            packed_ids.astype(jnp.bfloat16), "col", split_axis=0, concat_axis=0, tiled=True
        ).astype(packed_ids.dtype),
    )
    unpack = (got_ids[None, :] == request_ids[:, None]).astype(jnp.float32)
    phi_query = feature_map(query_heads.astype(jnp.float32))
    phi_select = jnp.einsum(
        "rp,rnhf->pnhf",
        unpack.astype(jnp.bfloat16),
        phi_query.astype(jnp.bfloat16),
        preferred_element_type=jnp.float32,
    ).astype(jnp.bfloat16)
    phi_full = jnp.einsum("rp,rnhf->pnhf", unpack, phi_query, precision=highest)
    slot_num = jnp.einsum(
        "pnhf,phfd->pnhd", phi_select, got_states, preferred_element_type=jnp.float32
    )
    slot_den = jnp.einsum("pnhf,phf->pnh", phi_full, got_norms, precision=highest)
    pref_num = jnp.einsum("rp,pnhd->rnhd", unpack, slot_num, precision=highest)
    pref_den = jnp.einsum("rp,pnh->rnh", unpack, slot_den, precision=highest)
    mixed = ((pref_num + tree_num) / (pref_den + tree_den)[..., None]).astype(jnp.bfloat16)
    mixed = mixed.reshape(tok_local, local_heads * value_width)
    partial_value = jnp.dot(mixed, w_out, preferred_element_type=jnp.float32)
    feature_count = partial_value.shape[1]
    share = feature_count // row_count
    attn_all = lax.psum(partial_value.astype(jnp.bfloat16), "row").astype(jnp.float32)
    residual_all = hidden + attn_all
    normed_mlp = rms_norm(residual_all, mlp_gain).astype(jnp.bfloat16)
    residual = lax.dynamic_slice_in_dim(residual_all, row_index * share, share, 1)
    gate_proj = jnp.dot(normed_mlp, w_gate, preferred_element_type=jnp.float32)
    up_proj = jnp.dot(normed_mlp, w_up, preferred_element_type=jnp.float32)
    activated = (jax.nn.silu(gate_proj) * up_proj).astype(jnp.bfloat16)
    mlp_share = lax.psum_scatter(
        jnp.einsum("fd,tf->dt", w_down, activated, preferred_element_type=jnp.float32).astype(
            jnp.bfloat16
        ),
        "row",
        scatter_dimension=0,
        tiled=True,
    ).astype(jnp.float32)
    hidden_out = (residual + jnp.transpose(mlp_share)).astype(jnp.bfloat16)
    node_ids = jnp.arange(nodes, dtype=jnp.int32)
    chosen = (node_ids[None, :] == accepted[:, None]).astype(jnp.float32)
    path_mask = jnp.einsum("ri,rij->rj", chosen, reached, precision=highest)
    phi_key = feature_map(key_heads.astype(jnp.float32))
    new_norms = jnp.einsum("rj,rjhf->rhf", path_mask, phi_key, precision=highest)
    weighted = phi_key.astype(jnp.bfloat16) * path_mask.astype(jnp.bfloat16)[:, :, None, None]
    new_states = jnp.einsum(
        "rjhf,rjhd->rhfd", weighted, value_heads, preferred_element_type=jnp.float32
    ).astype(jnp.bfloat16)
    return (hidden_out, new_states, new_norms)

MESH_KEYS = ("row", "col")


def picks(heads, feat_width, order, length):
    unit = heads * feat_width
    first = np.zeros((length, 128), np.float32)
    second = np.zeros((length, 128), np.float32)
    for h in range(heads):
        for f in range(1 + feat_width + feat_width * feat_width):
            if f == 0:
                a, b = unit + h, unit + h
            elif f <= feat_width:
                a, b = h * feat_width + f - 1, unit + h
            else:
                i, j = divmod(f - 1 - feat_width, feat_width)
                a, b = h * feat_width + i, h * feat_width + j
            first[order(f, h), a] = 1.0
            second[order(f, h), b] = 1.0
    return first, second


def feature_scale(feature, feat_width):
    square = (2.0 * feat_width) ** (-0.5)
    linear = feat_width ** (-0.25)
    return jnp.where(feature == 0, 1.0, jnp.where(feature <= feat_width, linear, square))


def peers_of(axis):
    size, me = lax.axis_size(axis), lax.axis_index(axis)
    return [lax.rem(me + step, size) for step in range(1, size)]


def greet(between):
    barrier = pltpu.get_barrier_semaphore()
    count = 0
    for axis in MESH_KEYS:
        for peer in peers_of(axis):
            pl.semaphore_signal(
                barrier, inc=1, device_id={axis: peer}, device_id_type=pl.DeviceIdType.MESH
            )
            count += 1
    between()
    pl.semaphore_wait(barrier, count)


def push(axis, peers, source_of, target, send_sem, recv_sem, base=0):
    copies = []
    for step, peer in enumerate(peers):
        copy = pltpu.make_async_remote_copy(
            src_ref=source_of(step, peer),
            dst_ref=target,
            send_sem=send_sem.at[base + step],
            recv_sem=recv_sem.at[base + step],
            device_id={axis: peer},
            device_id_type=pl.DeviceIdType.MESH,
        )
        copy.start()
        copies.append(copy)
    return copies


def extended(rows_t, heads):
    unit, tokens = rows_t.shape
    ids = lax.broadcasted_iota(jnp.int32, (128 - unit, tokens), 0)
    ones = jnp.where(ids < heads, 1.0, 0.0).astype(jnp.bfloat16)
    return jnp.concatenate([rows_t, ones], axis=0)


def dot(a, b, contract=(1, 0)):
    return lax.dot_general(
        a, b, (((contract[0],), (contract[1],)), ((), ())), preferred_element_type=jnp.float32
    )


def layer_kernel(
    heads, feat_width, features, value_width, requests, capacity,
    home_ref, request_ref, accepted_ref, hidden_ref, gain_ref, mlp_gain_ref, norms_ref, parent_ref,
    first_any, second_any, first_t_any, second_t_any, first_h_any, second_h_any,
    wq_any, wk_any, wv_any, states_any, wout_any, wgate_any, wup_any, wdown_any,
    out_ref, states_out, norms_out,
    wq, wk, wv, states, wout, wgate, wup, wdown,
    first_ref, second_ref, first_t_ref, second_t_ref, first_h_ref, second_h_ref, table, norms_flat, normed_mlp, head_mask,
    hid_t, normed, q_mine, q_all, k_mine, v_mine, spread, phi_all, nums,
    pair_out, pair_in, chip_out, chip_in,
    hid, stacked, sums, parts, gathered, blocks, kept, arrived,
    w_sem, hs_sem, hr_sem, qs_sem, qr_sem, bs_sem, br_sem, cs_sem, cr_sem,
    as_sem, ar_sem, gs_sem, gr_sem, ms_sem, mr_sem,
):
    bf16, f32 = jnp.bfloat16, jnp.float32
    me_row, me_col = lax.axis_index("row"), lax.axis_index("col")
    row_count, col_count = lax.axis_size("row"), lax.axis_size("col")
    chips = col_count // 2
    me_chip, me_core = me_col // 2, lax.rem(me_col, 2)
    tokens, width = hid.shape
    nodes = tokens // requests
    unit = heads * feat_width
    span = heads * nodes
    count = heads * features
    window = phi_all.shape[2]
    slots = norms_ref.shape[0]
    loads = [
        pltpu.make_async_copy(src, dst, w_sem.at[i])
        for i, (src, dst) in enumerate(
            (
                (wq_any, wq), (wk_any, wk), (wv_any, wv), (states_any, states),
                (wout_any, wout), (wgate_any, wgate), (wup_any, wup), (wdown_any, wdown),
                (first_any, first_ref), (second_any, second_ref),
                (first_t_any, first_t_ref), (second_t_any, second_t_ref),
                (first_h_any, first_h_ref), (second_h_any, second_h_ref),
            )
        )
    ]

    def start_loads():
        for i in (0, 1, 2, 8, 9, 3, 10, 11, 12, 13, 4, 5, 6, 7):
            loads[i].start()

    greet(start_loads)

    share = hidden_ref.shape[0]
    mine = hid_t.at[pl.ds(pl.multiple_of(me_row * share, 16), share)]
    hidden_copies = push("row", peers_of("row"), lambda i, p: hidden_ref, mine, hs_sem, hr_sem)
    mine[...] = hidden_ref[...]

    gain_t = jnp.transpose(gain_ref[...])
    for slot in range(slots):
        norms_flat[slot * heads : (slot + 1) * heads, :] = norms_ref[slot]
    norms = norms_flat[...]
    f_of = lax.broadcasted_iota(jnp.int32, (features, window), 0)
    t_of = lax.broadcasted_iota(jnp.int32, (features, window), 1)
    expand = jnp.where(t_of // heads == f_of, 1.0, 0.0).astype(bf16)
    top = norms.astype(bf16)
    rest = norms - top.astype(f32)
    middle = rest.astype(bf16)
    low = (rest - middle.astype(f32)).astype(bf16)
    wide = (dot(top, expand) + dot(middle, expand)) + dot(low, expand)
    row_head = lax.broadcasted_iota(jnp.int32, wide.shape, 0) % heads
    lane_head = lax.broadcasted_iota(jnp.int32, wide.shape, 1) % heads
    spread[...] = jnp.where(row_head == lane_head, wide, 0.0)

    row_ids = lax.broadcasted_iota(jnp.int32, (tokens, tokens), 0)
    lane_ids = lax.broadcasted_iota(jnp.int32, (tokens, tokens), 1)
    parent_row = jnp.concatenate(
        [parent_ref[r : r + 1, :] + r * nodes for r in range(requests)], axis=1
    )
    linked = jnp.logical_or(parent_row == row_ids, row_ids == lane_ids)
    reached = jnp.where(linked, 1.0, 0.0)
    for repeat in range(max(1, (nodes - 1).bit_length())):
        reached_low = reached.astype(bf16)
        reached = jnp.minimum(dot(reached_low, reached_low), 1.0)
    reached = jnp.transpose(reached)

    mask_lane = lax.broadcasted_iota(jnp.int32, (nodes, window), 1) % heads
    for h in range(heads):
        head_mask[h] = jnp.where(mask_lane == h, 1.0, 0.0).astype(bf16)

    homes = [home_ref[slot] for slot in range(slots)]
    places = []
    for slot in range(slots):
        rank = jnp.int32(0)
        for earlier in range(slot):
            rank += (homes[earlier] == homes[slot]).astype(jnp.int32)
        places.append(homes[slot] * capacity + rank)
    for place in range(col_count * capacity):
        found = jnp.int32(slots)
        for slot in range(slots):
            found += (places[slot] == place).astype(jnp.int32) * (slot - slots)
        table[place] = found

    for copy in hidden_copies:
        copy.wait_recv()
    total = jnp.zeros((1, tokens), f32)
    for j in range(width // 128):
        x = hid_t[128 * j : 128 * j + 128, :].astype(f32)
        total += jnp.sum(x * x, axis=0, keepdims=True)
    inverse = lax.rsqrt(total / width + epsilon)
    for j in range(width // 128):
        x = hid_t[128 * j : 128 * j + 128, :].astype(f32)
        normed[128 * j : 128 * j + 128, :] = (x * inverse * gain_t[:, j : j + 1]).astype(bf16)
    loads[0].wait()
    q_mine[...] = dot(wq[...], normed[...]).astype(bf16)
    q_copies = push("col", peers_of("col"), lambda i, p: q_mine, q_all.at[me_col], qs_sem, qr_sem)
    q_all[me_col] = q_mine[...]
    loads[1].wait()
    k_mine[...] = dot(wk[...], normed[...]).astype(bf16)
    loads[2].wait()
    v_mine[...] = dot(wv[...], normed[...]).astype(bf16)
    for j in range(width // 128):
        block = hid_t[128 * j : 128 * j + 128, :].astype(f32)
        hid[:, 128 * j : 128 * j + 128] = jnp.transpose(block)


    loads[8].wait()
    loads[9].wait()
    cuts = [(lo, min(lo + 384, window)) for lo in range(0, window, 384)]
    lane_feature = lax.broadcasted_iota(jnp.int32, (1, window), 1) // heads
    lane_scale = feature_scale(lane_feature, feat_width)

    def features_of(home):
        ext = extended(q_all[home], heads)
        for lo, hi in cuts:
            a = dot(ext, first_ref[:, lo:hi], (0, 0))
            b = dot(ext, second_ref[:, lo:hi], (0, 0))
            phi = a * b * lane_scale[:, lo:hi]
            for r in range(requests):
                phi_all[home * requests + r, :, lo:hi] = phi[r * nodes : (r + 1) * nodes, :]

    features_of(me_col)
    for step, copy in enumerate(q_copies):
        copy.wait()
        features_of(lax.rem(me_col + col_count - (step + 1), col_count))

    loads[3].wait()
    group = 16 // math.gcd(count, 16)
    nums[slots] = jnp.zeros((span, 128), f32)

    def slots_of(g, carry):
        norm_rows = spread[pl.ds(pl.multiple_of(g * (group * heads), 8), group * heads), :]
        for i in range(group):
            slot = g * group + i
            shift = (count * i) % 16
            start = count * i - shift
            owner = home_ref[slot] * requests + request_ref[slot]
            phi = phi_all[owner]
            norm_row = jnp.sum(norm_rows[i * heads : (i + 1) * heads, :], axis=0, keepdims=True)
            weighted = phi * norm_row
            weigh = weighted[:, 0:128]
            for lo in range(128, window, 128):
                weigh += weighted[:, lo : lo + 128]
            lane = lax.broadcasted_iota(jnp.int32, weigh.shape, 1) % heads
            den = [
                jnp.sum(jnp.where(lane == h, weigh, 0.0), axis=1, keepdims=True) for h in range(heads)
            ]
            if shift:
                phi = pltpu.roll(phi, shift, 1)
            phi = phi.astype(bf16)
            num = jnp.zeros((span, value_width), f32)
            reach = -(-(count + shift) // 16) * 16
            for lo, hi in [(lo, min(lo + 384, reach)) for lo in range(0, reach, 384)]:
                masked = jnp.concatenate(
                    [phi[:, lo:hi] * head_mask[h, :, lo:hi] for h in range(heads)], axis=0
                )
                rows = pl.ds(pl.multiple_of(g * (group * count) + start + lo, 16), hi - lo)
                num += dot(masked, states[rows, :])
            nums[slot, :, 0:value_width] = num
            nums[slot, :, value_width : value_width + 1] = jnp.concatenate(den, axis=0)
        return carry

    lax.fori_loop(0, slots // group, slots_of, 0)

    def home_sum(home, request):
        acc = jnp.zeros((span, 128), f32)
        for k in range(capacity):
            slot = table[home * capacity + k]
            wanted = jnp.full((span, 128), request_ref[jnp.minimum(slot, slots - 1)], jnp.int32)
            acc += jnp.where(wanted == request, nums[slot], 0.0)
        return acc

    for chip in range(chips):
        for r in range(requests):
            pair_out[chip, r * span : (r + 1) * span, :] = home_sum(2 * chip + (1 - me_core), r).astype(bf16)
    pair_copies = push(
        "col", [2 * me_chip + (1 - me_core)], lambda i, p: pair_out, pair_in, bs_sem, br_sem
    )

    k_ext = extended(k_mine[...], heads)
    tree_num, tree_den = [], []
    for h in range(heads):
        at = slice(h * feat_width, (h + 1) * feat_width)
        scaled = dot(q_mine[at, :], k_mine[at, :], (0, 0)) / math.sqrt(feat_width)
        kernel = (1.0 + scaled + 0.5 * scaled * scaled) * reached
        tree_den.append(jnp.sum(kernel, axis=1, keepdims=True))
        tree_num.append(
            dot(kernel.astype(bf16), v_mine[h * value_width : (h + 1) * value_width, :], (1, 1))
        )
    for copy in pair_copies:
        copy.wait()

    def combined(chip, r):
        got = pair_in[chip, r * span : (r + 1) * span, :].astype(f32)
        return home_sum(2 * chip + me_core, r) + got

    chip_peers = [lax.rem(me_chip + step, chips) for step in range(1, chips)]
    chip_copies = []
    for r in range(requests):
        for step, chip in enumerate(chip_peers):
            chip_out[r, step] = combined(chip, r).astype(bf16)
            chip_copies += push(
                "col", [2 * chip + me_core], lambda i, p: chip_out.at[r, step], chip_in.at[r, step],
                cs_sem, cr_sem, r * (chips - 1) + step,
            )
    pref = [combined(me_chip, r) for r in range(requests)]

    token_share = nodes // row_count
    steps = row_count - 1
    row_peers = peers_of("row")
    rows_of = lambda row: pl.ds(pl.multiple_of(row * token_share, 16), token_share)
    loads[4].wait()
    sum_copies = []
    for r in range(requests):
        for step in range(chips - 1):
            chip_copies[r * (chips - 1) + step].wait()
            pref[r] += chip_in[r, step].astype(f32)
        partial = jnp.zeros((nodes, width), f32)
        for h in range(heads):
            rows = pref[r][h * nodes : (h + 1) * nodes, :]
            at = slice(r * nodes, (r + 1) * nodes)
            num = rows[:, 0:value_width] + tree_num[h][at, :]
            den = rows[:, value_width : value_width + 1] + tree_den[h][at, :]
            mixed = (num / den).astype(bf16)
            partial += dot(mixed, wout[h * value_width : (h + 1) * value_width, :])
        sums[r] = partial.astype(bf16)
        sum_copies.append(
            push(
                "row", row_peers, lambda i, p: sums.at[r, rows_of(p)], parts.at[r, me_row],
                as_sem, ar_sem, r * steps,
            )
        )
        parts[r, me_row] = sums[r, rows_of(me_row), :]

    for i in range(10, 14):
        loads[i].wait()
    pick_row = lax.broadcasted_iota(jnp.int32, (16, tokens), 0)
    pick_lane = lax.broadcasted_iota(jnp.int32, (16, tokens), 1)
    chosen = jnp.zeros((16, tokens), f32)
    for r in range(requests):
        hit = jnp.logical_and(pick_row == r, pick_lane == accepted_ref[r] + r * nodes)
        chosen = jnp.where(hit, 1.0, chosen)
    path = dot(chosen.astype(bf16), reached.astype(bf16))
    path_low = path.astype(bf16)
    stride = first_h_ref.shape[0] // heads
    for h in range(heads):
        at = slice(h * stride, (h + 1) * stride)
        feature = lax.broadcasted_iota(jnp.int32, (stride, tokens), 0)
        phi = dot(first_h_ref[at, :], k_ext) * dot(second_h_ref[at, :], k_ext)
        phi = phi * feature_scale(feature, feat_width)
        high = phi.astype(bf16)
        low = (phi - high.astype(f32)).astype(bf16)
        norm = dot(path_low, high, (1, 1)) + dot(path_low, low, (1, 1))
        for r in range(requests):
            norms_out[r, h : h + 1, :] = norm[r : r + 1, 0:features]
    phi = dot(first_t_ref[...], k_ext) * dot(second_t_ref[...], k_ext)
    t = lax.broadcasted_iota(jnp.int32, phi.shape, 0)
    high = (phi * feature_scale(t // heads, feat_width)).astype(bf16).astype(f32)
    for h in range(heads):
        values = v_mine[h * value_width : (h + 1) * value_width, :].astype(f32)
        stacked[h * tokens : (h + 1) * tokens, :] = jnp.transpose(values).astype(bf16)
    def accepted_page(r):
        weighted = high * path[r : r + 1, :]
        wide = jnp.concatenate(
            [jnp.where(t % heads == h, weighted, 0.0).astype(bf16) for h in range(heads)], axis=1
        )
        page = dot(wide, stacked[...])
        states_out[r * count : (r + 1) * count, :] = page[0:count, :].astype(bf16)

    accepted_page(0)

    gather_copies = []
    for r in range(requests):
        for copy in sum_copies[r]:
            copy.wait()
        attn = parts[r, 0].astype(f32)
        for g in range(1, row_count):
            attn += parts[r, g].astype(f32)
        gathered[r, rows_of(me_row), :] = attn.astype(bf16)
        mine = gathered.at[r, rows_of(me_row)]
        gather_copies.append(
            push("row", row_peers, lambda i, p: mine, mine, gs_sem, gr_sem, r * steps)
        )

    for r in range(1, requests):
        accepted_page(r)

    mlp_copies = []
    for r in range(requests):
        for copy in gather_copies[r]:
            copy.wait()
        residual = hid[r * nodes : (r + 1) * nodes, :] + gathered[r].astype(f32)
        for g in range(row_count):
            kept[r, g] = residual[:, g * share : (g + 1) * share]
        inverse = lax.rsqrt(jnp.sum(residual * residual, axis=1, keepdims=True) / width + epsilon)
        for j in range(width // 128):
            at = slice(128 * j, 128 * j + 128)
            scaled = residual[:, at] * inverse * mlp_gain_ref[j : j + 1, :]
            normed_mlp[r, :, at] = scaled.astype(bf16)
        if r == 0:
            loads[5].wait()
        gate = dot(normed_mlp[r], wgate[...])
        if r == 0:
            loads[6].wait()
        up = dot(normed_mlp[r], wup[...])
        active = (gate / (1.0 + jnp.exp(-gate)) * up).astype(bf16)
        if r == 0:
            loads[7].wait()
        mlp = dot(active, wdown[...])
        for g in range(row_count):
            blocks[r, g] = mlp[:, g * share : (g + 1) * share].astype(bf16)
        mlp_copies.append(
            push(
                "row", row_peers, lambda i, p: blocks.at[r, p], arrived.at[r, me_row],
                ms_sem, mr_sem, r * steps,
            )
        )
        arrived[r, me_row] = blocks[r, me_row]
    finals = []
    for r in range(requests):
        for copy in mlp_copies[r]:
            copy.wait()
        final = kept[r, me_row]
        for g in range(row_count):
            final += arrived[r, g].astype(f32)
        finals.append(final)
    final = jnp.concatenate(finals, axis=0)
    for lo in range(0, share, 128):
        hi = min(lo + 128, share)
        out_ref[lo:hi, :] = jnp.transpose(final[:, lo:hi]).astype(bf16)
    for copy in hidden_copies:
        copy.wait_send()


def kernel_local(
    hidden_in, attn_gain, mlp_gain, w_query, w_key, w_value, w_out, w_gate, w_up, w_down,
    page_states, page_norms, page_home, page_request, parents, accepted,
):
    slots, heads, features, value_width = page_states.shape
    feat_width = w_query.shape[1] // heads
    requests, nodes = parents.shape
    tokens, share = hidden_in.shape
    width = w_gate.shape[0]
    rows, cols = lax.axis_size("row"), lax.axis_size("col")
    capacity = max(2, 2 * slots // cols)
    bf16, f32 = jnp.bfloat16, jnp.float32
    vmem = pl.BlockSpec(memory_space=pltpu.VMEM)
    smem = pl.BlockSpec(memory_space=pltpu.SMEM)
    hbm = pl.BlockSpec(memory_space=pl.ANY)
    dma = pltpu.SemaphoreType.DMA
    unit = heads * feat_width
    span = heads * nodes
    count = heads * features
    window = -(-(count + 16) // 128) * 128

    state_rows = jnp.transpose(page_states, (0, 2, 1, 3)).reshape(slots * count, value_width)
    first, second = picks(heads, feat_width, lambda f, h: f * heads + h, window)
    stride = -(-features // 16) * 16
    first_h, second_h = picks(heads, feat_width, lambda f, h: h * stride + f, heads * stride)
    constants = [jnp.asarray(c, bf16) for c in (first.T, second.T, first, second, first_h, second_h)]
    token_share = nodes // rows
    chips = cols // 2
    hidden_out, state_out, norm_out = pl.pallas_call(
        functools.partial(layer_kernel, heads, feat_width, features, value_width, requests, capacity),
        out_shape=(
            jax.ShapeDtypeStruct((share, tokens), bf16),
            jax.ShapeDtypeStruct((requests * count, value_width), bf16),
            jax.ShapeDtypeStruct((requests, heads, features), f32),
        ),
        in_specs=[smem] * 3 + [vmem] * 5 + [hbm] * 14,
        out_specs=(vmem,) * 3,
        scratch_shapes=[
            pltpu.VMEM((unit, width), bf16),
            pltpu.VMEM((unit, width), bf16),
            pltpu.VMEM((heads * value_width, width), bf16),
            pltpu.VMEM(state_rows.shape, bf16),
            pltpu.VMEM(w_out.shape, bf16),
            pltpu.VMEM(w_gate.shape, bf16),
            pltpu.VMEM(w_up.shape, bf16),
            pltpu.VMEM(w_down.shape, bf16),
        ]
        + [pltpu.VMEM(c.shape, bf16) for c in constants]
        + [
            pltpu.SMEM((cols * capacity,), jnp.int32),
            pltpu.VMEM((slots * heads, features), f32),
            pltpu.VMEM((requests, nodes, width), bf16),
            pltpu.VMEM((heads, nodes, window), bf16),
            pltpu.VMEM((width, tokens), bf16),
            pltpu.VMEM((width, tokens), bf16),
            pltpu.VMEM((unit, tokens), bf16),
            pltpu.VMEM((cols, unit, tokens), bf16),
            pltpu.VMEM((unit, tokens), bf16),
            pltpu.VMEM((heads * value_width, tokens), bf16),
            pltpu.VMEM((slots * heads, window), f32),
            pltpu.VMEM((cols * requests, nodes, window), f32),
            pltpu.VMEM((slots + 1, span, 128), f32),
            pltpu.VMEM((chips, requests * span, 128), bf16),
            pltpu.VMEM((chips, requests * span, 128), bf16),
            pltpu.VMEM((requests, chips - 1, span, 128), bf16),
            pltpu.VMEM((requests, chips - 1, span, 128), bf16),
            pltpu.VMEM((tokens, width), f32),
            pltpu.VMEM((heads * tokens, value_width), bf16),
            pltpu.VMEM((requests, nodes, width), bf16),
            pltpu.VMEM((requests, rows, token_share, width), bf16),
            pltpu.VMEM((requests, nodes, width), bf16),
            pltpu.VMEM((requests, rows, nodes, share), bf16),
            pltpu.VMEM((requests, rows, nodes, share), f32),
            pltpu.VMEM((requests, rows, nodes, share), bf16),
            dma((14,)),
            dma((rows - 1,)),
            dma((rows - 1,)),
            dma((cols - 1,)),
            dma((cols - 1,)),
            dma((1,)),
            dma((1,)),
            dma((requests * (chips - 1),)),
            dma((requests * (chips - 1),)),
        ]
        + [dma((requests * (rows - 1),))] * 6,
        compiler_params=pltpu.CompilerParams(
            collective_id=0, has_side_effects=True, vmem_limit_bytes=58 * 1024 * 1024
        ),
        name="layer",
    )(
        page_home[:, 0], page_request, accepted, hidden_in.T, attn_gain.reshape(width // 128, 128),
        mlp_gain.reshape(width // 128, 128), page_norms, parents, *constants,
        w_query.T, w_key.T, w_value.T, state_rows, w_out, w_gate, w_up, w_down,
    )
    new_states = jnp.transpose(state_out.reshape(requests, features, heads, value_width), (0, 2, 1, 3))
    return (hidden_out.T, new_states, norm_out)


def kernels_fit(*arrays):
    hidden_in, w_query, page_states, parents = arrays[0], arrays[3], arrays[10], arrays[14]
    slots, heads, features, value_width = page_states.shape
    tokens, rows = hidden_in.shape[0], lax.axis_size("row")
    group = 16 // math.gcd(heads * features, 16)
    return (
        tokens == 128
        and parents.shape[1] % (16 * rows) == 0
        and hidden_in.shape[1] % 16 == 0
        and 128 % heads == 0
        and (group == 1 or 16 % heads == 0)
        and (group * heads) % 8 == 0
        and w_query.shape[1] + heads <= 128
        and value_width < 128
        and value_width % 16 == 0
        and slots % group == 0
        and parents.shape[0] <= 16
        and lax.axis_size("col") % 2 == 0
        and lax.axis_size("col") > 2
    )


def on_device(*arrays):
    return kernel_local(*arrays) if kernels_fit(*arrays) else local(*arrays)


def solution(mesh):
    return jax.shard_map(
        on_device,
        mesh=mesh,
        in_specs=(
            P("col", "row"),
            P(),
            P(),
            P(None, "row"),
            P(None, "row"),
            P(None, "row"),
            P("row", None),
            P(None, "row"),
            P(None, "row"),
            P("row", None),
            P("col", "row", None, None),
            P("col", "row", None),
            P("col", None),
            P("col"),
            P("col", None),
            P("col"),
        ),
        out_specs=(P("col", "row"), P("col", "row", None, None), P("col", "row", None)),
        check_vma=False,
    )
```
